512 devices in a mesh: ctx: 64 (over z, y_lo, core), head: 8 (over y_hi, x).
Axes of the slice: x: 4, y: 4 (y_hi: 2, y_lo: 2; y = y_hi * 2 + y_lo), z: 16, core: 2. Of those that a mesh axis runs over, the one named last changes fastest.
Arguments:
- queries: float32 [2, 64, 64, 128], P(None, 'ctx', 'head'), may hold values from -256 to 256
- prompt_keys: float32 [16384, 8, 128], P('ctx', 'head'), may hold values from -6 to 6
- prompt_values: float32 [16384, 8, 128], P('ctx', 'head'), may hold values from -6 to 6
- suffix_keys: float32 [64, 128, 8, 128], P('ctx', None, 'head'), may hold values from -8.4 to 8.4
- suffix_values: float32 [64, 128, 8, 128], P('ctx', None, 'head'), may hold values from -6 to 6
- new_keys: float32 [2, 64, 8, 128], P(None, 'ctx', 'head'), may hold values from -18 to 18
- new_values: float32 [2, 64, 8, 128], P(None, 'ctx', 'head'), may hold values from -6 to 6
- suffix_lengths: int32 [64], P('ctx'), may hold values from 1 to 128, as said below
- out_weight: float32 [8192, 5120], P('head', 'ctx'), may hold values from -0.0625 to 0.0625
Outputs:
- layer_out: float32 [2, 64, 5120], P(None, 'head', 'ctx')
The draws below stay inside these ranges and needn't reach their ends.
Inputs may be any that keep to these rules, and one draw needn't show every extreme that they name: `suffix_lengths`: some row has exactly 128 live slots.
All inputs are finite; a program needn't handle non-finite values.
Results may differ from the reference program's by a relative error of at most 0.0003.
Values sent between devices are 32-bit elements; how exact they have to be, the bound alone decides.
A program may use at most 192 MiB of HBM per device.

```python
import jax
import jax.numpy as jnp
from jax import lax

QH = 64
KVH = 8
HD = 128
D = 5120
SUF = 128
STEPS = 2
ROWS = 64
PROMPT = 16384


def draw_queries(key, part):
    key = jax.random.fold_in(key, 1)
    full_shape = (STEPS, ROWS, QH, HD)
    return jnp.clip(3.0 * jax.random.normal(key, full_shape, jnp.float32), -24.0, 24.0)


def draw_prompt_keys(key, part):
    key = jax.random.fold_in(key, 2)
    full_shape = (PROMPT, KVH, HD)
    return jnp.clip(jax.random.normal(key, full_shape, jnp.float32), -6.0, 6.0)


def draw_suffix_lengths(key, part):
    key = jax.random.fold_in(key, 3)
    length_key, spot_key = jax.random.split(key)
    lengths = jax.random.randint(length_key, (ROWS,), 1, SUF + 1, jnp.int32)
    full_row = jax.random.randint(spot_key, (), 0, ROWS, jnp.int32)
    return lengths.at[full_row].set(SUF)


def shard_levels(own_key, extent, cuts, smallest, high):
    factor_of, own = 1.0, jax.random.fold_in(own_key, 6)
    for axis_at, shards_of in cuts:
        draws = jnp.exp(jax.random.uniform(jax.random.fold_in(own, axis_at), (shards_of,), jnp.float32, smallest / len(cuts), high / len(cuts)))
        factor_of = factor_of * jnp.repeat(draws, extent[axis_at] // shards_of).reshape([-1 if axis == axis_at else 1 for axis in range(len(extent))])
    return factor_of


def bell_draw(rng, extent, width, limit, cuts=(), kind=jnp.bfloat16):
    array = width * jax.random.normal(rng, extent, jnp.float32)
    if cuts:
        array = array * shard_levels(rng, extent, cuts, -0.22, 0.18)
    return jnp.clip(array, -limit, limit).astype(kind)


def setup_inputs(seed: int = 0) -> dict:
    splits = jax.random.split(jax.random.key(seed), 10)
    queries = draw_queries(jax.random.fold_in(splits[9], 71), 0)
    prompt_keys = draw_prompt_keys(jax.random.fold_in(splits[9], 71), 0)
    prompt_values = bell_draw(splits[2], (PROMPT, KVH, HD), 1.0, 6.0, ((0, 64), (1, 8)), jnp.float32)
    suffix_keys = bell_draw(splits[3], (ROWS, SUF, KVH, HD), 1.4, 8.4, ((0, 64), (2, 8)), jnp.float32)
    suffix_values = bell_draw(splits[4], (ROWS, SUF, KVH, HD), 1.0, 6.0, ((0, 64), (2, 8)), jnp.float32)
    new_keys = bell_draw(splits[5], (STEPS, ROWS, KVH, HD), 3.0, 18.0, ((1, 64), (2, 8)), jnp.float32)
    new_values = bell_draw(splits[6], (STEPS, ROWS, KVH, HD), 1.0, 6.0, ((1, 64), (2, 8)), jnp.float32)
    suffix_lengths = draw_suffix_lengths(jax.random.fold_in(splits[9], 71), 0)
    out_weight = bell_draw(splits[8], (QH * HD, D), (QH * HD) ** -0.5, 0.0625, ((0, 8), (1, 64)), jnp.float32)
    return {"queries": queries, "prompt_keys": prompt_keys, "prompt_values": prompt_values, "suffix_keys": suffix_keys, "suffix_values": suffix_values, "new_keys": new_keys, "new_values": new_values, "suffix_lengths": suffix_lengths, "out_weight": out_weight}


HIGHEST = lax.Precision.HIGHEST


def combine(first, second):
    peak_a, total_a, weighted_a = first
    peak_b, total_b, weighted_b = second
    row_peak = jnp.maximum(peak_a, peak_b)
    scale_a = jnp.exp(peak_a - row_peak)
    scale_b = jnp.exp(peak_b - row_peak)
    return (row_peak, total_a * scale_a + total_b * scale_b,
            weighted_a * scale_a[..., None] + weighted_b * scale_b[..., None])


def prompt_part(query_block, key_rows, value_rows):
    score_scale = query_block.shape[-1] ** -0.5
    scores = jnp.einsum("trkgd,pkd->trkgp", query_block, key_rows, precision=HIGHEST) * score_scale
    row_peak = jnp.max(scores, axis=-1)
    weights = jnp.exp(scores - row_peak[..., None])
    row_total = jnp.sum(weights, axis=-1)
    weighted = jnp.einsum("trkgp,pkd->trkgd", weights, value_rows, precision=HIGHEST)
    return row_peak, row_total, weighted


def suffix_part(query_block, suf_keys, suf_values, fresh_keys, fresh_values, lengths):
    score_scale = query_block.shape[-1] ** -0.5
    slot_count = suf_keys.shape[1]
    step_count = query_block.shape[0]
    suf_scores = jnp.einsum("trkgd,rskd->trkgs", query_block, suf_keys, precision=HIGHEST) * score_scale
    live_slots = jnp.arange(slot_count, dtype=jnp.int32)[None, :] < lengths[:, None]
    suf_scores = jnp.where(live_slots[None, :, None, None, :], suf_scores, -1e30)
    new_scores = jnp.einsum("trkgd,urkd->trkgu", query_block, fresh_keys, precision=HIGHEST) * score_scale
    step_ids = jnp.arange(step_count, dtype=jnp.int32)
    new_mask = step_ids[None, :] <= step_ids[:, None]
    new_scores = jnp.where(new_mask[:, None, None, None, :], new_scores, -1e30)
    row_peak = jnp.maximum(jnp.max(suf_scores, axis=-1), jnp.max(new_scores, axis=-1))
    suf_weights = jnp.exp(suf_scores - row_peak[..., None])
    new_weights = jnp.exp(new_scores - row_peak[..., None])
    row_total = jnp.sum(suf_weights, axis=-1) + jnp.sum(new_weights, axis=-1)
    weighted = (jnp.einsum("trkgs,rskd->trkgd", suf_weights, suf_values, precision=HIGHEST)
                + jnp.einsum("trkgu,urkd->trkgd", new_weights, fresh_values, precision=HIGHEST))
    return row_peak, row_total, weighted


def reference(queries, prompt_keys, prompt_values, suffix_keys, suffix_values, new_keys, new_values, suffix_lengths, out_weight):
    group_size = QH // KVH

    def one_row(items):
        query_row, suf_keys, suf_values, fresh_keys, fresh_values, length = items
        query_block = query_row.reshape(STEPS, 1, KVH, group_size, HD)
        suffix_parts = suffix_part(query_block, suf_keys[None], suf_values[None],
                                   fresh_keys[:, None], fresh_values[:, None], length.reshape(1))
        merged = combine(prompt_part(query_block, prompt_keys, prompt_values), suffix_parts)
        attention = merged[2] / merged[1][..., None]
        return attention.reshape(STEPS, QH * HD)

    per_row = lax.map(one_row, (jnp.moveaxis(queries, 1, 0), suffix_keys, suffix_values,
                                jnp.moveaxis(new_keys, 1, 0), jnp.moveaxis(new_values, 1, 0), suffix_lengths))
    attention = jnp.moveaxis(per_row, 0, 1)
    return jnp.einsum("tbf,fd->tbd", attention, out_weight, precision=HIGHEST)
```

```python
import jax
import jax.numpy as jnp
from jax import lax
from jax.experimental import pallas as pl
from jax.experimental.pallas import tpu as pltpu
from jax.sharding import PartitionSpec as P

MESH = pl.DeviceIdType.MESH
F32, BF16 = jnp.float32, jnp.bfloat16
Z, QUAD, HEADS = 16, 4, 8
WINDOW = 4
BLOCK = 16
HD = 128
NEAR = (12, 13, 14, 15, 0, 1, 2, 3)
FAR = (4, 5, 6, 7, 8, 9, 10, 11)
FAR_FIRST = sorted(range(1, Z), key=lambda d: -min(d, Z - d))


def nt(a, b):
    return lax.dot_general(a, b, (((1,), (1,)), ((), ())), preferred_element_type=F32)


def nn(a, b):
    return jnp.dot(a, b, preferred_element_type=F32)


def split2(x):
    high = x.astype(BF16)
    return high, (x - high.astype(F32)).astype(BF16)


def split3(x):
    high = x.astype(BF16)
    rest = x - high.astype(F32)
    middle = rest.astype(BF16)
    return high, middle, (rest - middle.astype(F32)).astype(BF16)


def kernel(
    q_in, k_in, v_in, sk_in, sv_in, nk_in, nv_in, len_in, w_in, out_ref,
    qbuf, kv, w, sk, sv, nk, nv, length, ka, kb, kc, vv, wh, wl,
    osend, orecv, lsend, lrecv, att, psend, precv,
    in_sem, a_send, a_recv, x_send, x_recv, o_send, o_recv, l_send, l_recv, c_send, c_recv, d_send, d_recv,
):
    ctx, head = lax.axis_index("ctx"), lax.axis_index("head")
    z, q = ctx // QUAD, lax.rem(ctx, QUAD)
    core, side = lax.rem(q, 2), q // 2

    def along(d):
        return (lax.rem(ctx + QUAD * (d % Z), Z * QUAD), head)

    def in_quad(k, d=0):
        c = 1 - core if k & 1 else core
        s = 1 - side if k & 2 else side
        return (z * QUAD + s * 2 + c, lax.rem(head + d, HEADS))

    def remote(src, dst, send, recv, to):
        return pltpu.make_async_remote_copy(
            src_ref=src, dst_ref=dst, send_sem=send, recv_sem=recv, device_id=to, device_id_type=MESH
        )

    window = [d for d in FAR_FIRST if min(d, Z - d) <= WINDOW]
    barrier = pltpu.get_barrier_semaphore()
    for d in window:
        pl.semaphore_signal(barrier, inc=1, device_id=along(d), device_id_type=MESH)
    mates = [(k, d) for d in (0, 2, 6, 4, 1, 3, 5, 7) for k in (2, 3, 1, 0) if (k, d) != (0, 0)]
    for k, d in mates:
        pl.semaphore_signal(barrier, inc=1, device_id=in_quad(k, d), device_id_type=MESH)

    own = [
        pltpu.make_async_copy(src, dst, in_sem.at[i])
        for i, (src, dst) in enumerate(
            (
                (q_in, qbuf.at[0]), (k_in, kv.at[0, 0]), (v_in, kv.at[0, 1]), (sk_in, sk), (sv_in, sv),
                (nk_in, nk), (nv_in, nv), (len_in, length), (w_in, w.at[0]),
            )
        )
    ]
    for c in own:
        c.start()
    pl.semaphore_wait(barrier, len(window) + len(mates))

    first = {d: remote(q_in, qbuf.at[Z - d], a_send.at[d], a_recv.at[d], along(d)) for d in window}
    for d in window:
        first[d].start()
    y_kv = [remote((k_in, v_in)[i], kv.at[2, i], x_send.at[i], x_recv.at[i], in_quad(2)) for i in (0, 1)]
    c_kv = [remote((k_in, v_in)[i], kv.at[1, i], x_send.at[2 + i], x_recv.at[2 + i], in_quad(1)) for i in (0, 1)]
    cy_kv = [remote(kv.at[2, i], kv.at[3, i], x_send.at[4 + i], x_recv.at[4 + i], in_quad(1)) for i in (0, 1)]
    y_w = remote(w_in, w.at[2], x_send.at[6], x_recv.at[6], in_quad(2))
    c_w = remote(w_in, w.at[1], x_send.at[7], x_recv.at[7], in_quad(1))
    cy_w = remote(w.at[2], w.at[3], x_send.at[8], x_recv.at[8], in_quad(1))
    for c in y_kv + c_kv:
        c.start()
    for c in own:
        c.wait()

    second = []
    for k in range(1, WINDOW + 1):
        first[Z - k].wait_recv()
        c = remote(qbuf.at[k], qbuf.at[k + WINDOW], a_send.at[Z + k], a_recv.at[Z + k], along(-WINDOW))
        c.start()
        second.append(c)
        first[k].wait_recv()
        if k < WINDOW:
            c = remote(
                qbuf.at[Z - k], qbuf.at[Z - k - WINDOW], a_send.at[Z + 8 + k], a_recv.at[Z + 8 + k], along(WINDOW)
            )
            c.start()
            second.append(c)

    def prepare(i):
        rows = pl.ds(i * 256, 256)
        high, middle, low = split3(kv[i, 0])
        ka[rows, :] = jnp.concatenate([high, high], axis=1)
        kb[rows, :] = jnp.concatenate([middle, middle], axis=1)
        kc[rows, :] = jnp.concatenate([low, high], axis=1)
        high, low = split2(kv[i, 1])
        vv[rows, :] = jnp.concatenate([high, low], axis=1)

    prepare(0)
    for c in c_kv:
        c.wait_recv()
    prepare(1)
    for i in (0, 1):
        y_kv[i].wait_recv()
        cy_kv[i].start()
    y_w.start()
    c_w.start()
    prepare(2)
    for c in cy_kv:
        c.wait_recv()
    prepare(3)

    scale = HD**-0.5
    lane = lax.broadcasted_iota(jnp.int32, (128, 128), 1)
    row = lax.broadcasted_iota(jnp.int32, (128, 128), 0)
    sends = []

    def prompt(b, slots):
        queries = jnp.concatenate([qbuf[s] for s in slots], axis=0)
        high, middle, low = split3(queries)
        qa = jnp.concatenate([high, middle], axis=1)
        qc = jnp.concatenate([high, low], axis=1)
        scores = nt(qa, ka[...]) + nt(qa, kb[...]) + nt(qc, kc[...])
        peak = jnp.max(scores, axis=1, keepdims=True)
        weights = jnp.exp((scores - peak) * scale)
        total = jnp.sum(weights, axis=1, keepdims=True)
        high, low = split2(weights)
        both = nn(high, vv[...]) + nn(low, vv[...])
        mixed = (both[:, :HD] + both[:, HD:]) / total
        logs = peak * scale + jnp.log(total)
        lsend[b] = jnp.sum(jnp.where(lane == row, logs, 0.0), axis=0, keepdims=True)
        for j, s in enumerate(slots):
            osend[s] = mixed[j * BLOCK : (j + 1) * BLOCK]
        for s in sorted(slots, key=lambda s: -min(s, Z - s)):
            if s:
                sends.append(remote(osend.at[s], orecv.at[Z - s], o_send.at[s], o_recv.at[s], along(s)))
                sends.append(remote(lsend.at[b], lrecv.at[Z - s], l_send.at[s], l_recv.at[s], along(s)))
                sends[-2].start()
                sends[-1].start()

    prompt(0, NEAR)
    for c in second:
        c.wait_recv()
    prompt(1, FAR)

    queries = qbuf[0]
    high, middle, low = split3(queries)
    kh, km, kl = split3(sk[...])
    scores = nt(high, kh) + nt(middle, kh) + nt(high, km) + nt(middle, km) + nt(high, kl) + nt(low, kh)
    lane16 = lax.broadcasted_iota(jnp.int32, (BLOCK, 128), 1)
    row16 = lax.broadcasted_iota(jnp.int32, (BLOCK, 128), 0)
    scores = jnp.where(lane16 < length[0], scores * scale, -1e30)
    fresh = nk[...]
    new0 = jnp.sum(queries * fresh[0:1], axis=1, keepdims=True) * scale
    new1 = jnp.sum(queries * fresh[1:2], axis=1, keepdims=True) * scale
    new1 = jnp.where(row16[:, :1] >= 8, new1, -1e30)
    peak = jnp.maximum(jnp.max(scores, axis=1, keepdims=True), jnp.maximum(new0, new1))
    weights, new0, new1 = jnp.exp(scores - peak), jnp.exp(new0 - peak), jnp.exp(new1 - peak)
    total = jnp.sum(weights, axis=1, keepdims=True) + new0 + new1
    wth, wtl = split2(weights)
    vh, vl = split2(sv[...])
    fresh = nv[...]
    mixed = nn(wth, vh) + nn(wth, vl) + nn(wtl, vh) + new0 * fresh[0:1] + new1 * fresh[1:2]
    parts = [(peak + jnp.log(total), mixed / total)]

    def columns(k):
        high, low = split2(w[k])
        wh[k, 0:80] = high
        wl[k, 0:80] = low
        wh[k, 80:128] = jnp.zeros((48, 1024), BF16)
        wl[k, 80:128] = jnp.zeros((48, 1024), BF16)

    columns(0)
    c_w.wait_recv()
    columns(1)
    y_w.wait_recv()
    cy_w.start()
    columns(2)
    cy_w.wait_recv()
    columns(3)

    def logs_of(values, j):
        return jnp.sum(jnp.where(lane16 == row16 + BLOCK * j, values, 0.0), axis=1, keepdims=True)

    parts.append((logs_of(lsend[0], NEAR.index(0)), osend[0]))
    for c in sends:
        c.wait_recv()
    for s in range(1, Z):
        mine = Z - s
        j = NEAR.index(mine) if mine in NEAR else FAR.index(mine)
        parts.append((logs_of(lrecv[s], j), orecv[s]))
    peak = parts[0][0]
    for logs, _ in parts[1:]:
        peak = jnp.maximum(peak, logs)
    total, mixed = jnp.zeros((BLOCK, 1), F32), jnp.zeros((BLOCK, HD), F32)
    for logs, value in parts:
        share = jnp.exp(logs - peak)
        total += share
        mixed += share * value
    mine = pl.ds(pl.multiple_of(z * BLOCK, BLOCK), BLOCK)
    att[mine, :] = mixed / total

    spread = [remote(att.at[mine], att.at[mine], c_send.at[d], c_recv.at[d], along(d)) for d in FAR_FIRST]
    for c in spread:
        c.start()
    for c in spread:
        c.wait_recv()

    rows = jnp.concatenate([att[pl.ds(g, 32, stride=8), :] for g in range(8)], axis=1)
    high, low = split2(rows)
    for k in range(QUAD):
        part = nt(high, wh[k]) + nt(low, wh[k]) + nt(high, wl[k])
        for h in range(HEADS):
            psend[k, h] = part[4 * h : 4 * h + 4]
    last = []
    for k, d in mates:
        last.append(
            remote(
                psend.at[k, lax.rem(head + d, HEADS)], precv.at[(HEADS - d) % HEADS, q],
                d_send.at[d * QUAD + k], d_recv.at[d * QUAD + k], in_quad(k, d),
            )
        )
        last[-1].start()
    precv[0, q] = psend[0, head]
    for c in last:
        c.wait_recv()
    summed = precv[0]
    for d in range(1, HEADS):
        summed += precv[d]
    for other in range(QUAD):
        for half in range(2):
            for t in range(2):
                out_ref[t, half * QUAD + other, :] = summed[other, half * 2 + t, :80]
    for c in list(first.values()) + second + y_kv + c_kv + cy_kv + [y_w, c_w, cy_w] + sends + spread + last:
        c.wait_send()


def local(
    queries, prompt_keys, prompt_values, suffix_keys, suffix_values, new_keys, new_values, suffix_lengths, out_weight
):
    dma = pltpu.SemaphoreType.DMA
    return pl.pallas_call(
        kernel,
        out_shape=jax.ShapeDtypeStruct((2, 8, 80), F32),
        in_specs=[pl.BlockSpec(memory_space=pltpu.HBM)] * 9,
        out_specs=pl.BlockSpec(memory_space=pltpu.VMEM),
        scratch_shapes=[
            pltpu.VMEM((Z, BLOCK, HD), F32),
            pltpu.VMEM((QUAD, 2, 256, HD), F32),
            pltpu.VMEM((QUAD, 80, 1024), F32),
            pltpu.VMEM((128, HD), F32),
            pltpu.VMEM((128, HD), F32),
            pltpu.VMEM((2, HD), F32),
            pltpu.VMEM((2, HD), F32),
            pltpu.SMEM((1,), jnp.int32),
            pltpu.VMEM((1024, 256), BF16),
            pltpu.VMEM((1024, 256), BF16),
            pltpu.VMEM((1024, 256), BF16),
            pltpu.VMEM((1024, 256), BF16),
            pltpu.VMEM((QUAD, 128, 1024), BF16),
            pltpu.VMEM((QUAD, 128, 1024), BF16),
            pltpu.VMEM((Z, BLOCK, HD), F32),
            pltpu.VMEM((Z, BLOCK, HD), F32),
            pltpu.VMEM((2, 1, HD), F32),
            pltpu.VMEM((Z, 1, HD), F32),
            pltpu.VMEM((Z * BLOCK, HD), F32),
            pltpu.VMEM((QUAD, HEADS, 4, 128), F32),
            pltpu.VMEM((HEADS, QUAD, 4, 128), F32),
            dma((9,)),
            dma((28,)), dma((28,)),
            dma((9,)), dma((9,)),
            dma((Z,)), dma((Z,)),
            dma((Z,)), dma((Z,)),
            dma((Z,)), dma((Z,)),
            dma((HEADS * QUAD,)), dma((HEADS * QUAD,)),
        ],
        compiler_params=pltpu.CompilerParams(
            collective_id=0, has_side_effects=True, vmem_limit_bytes=60 * 2**20
        ),
    )(
        queries.reshape(BLOCK, HD),
        prompt_keys.reshape(256, HD),
        prompt_values.reshape(256, HD),
        suffix_keys.reshape(128, HD),
        suffix_values.reshape(128, HD),
        new_keys.reshape(2, HD),
        new_values.reshape(2, HD),
        suffix_lengths,
        out_weight.T,
    )


def solution(mesh):
    return jax.shard_map(
        local,
        mesh=mesh,
        in_specs=(
            P(None, "ctx", "head", None),
            P("ctx", "head", None),
            P("ctx", "head", None),
            P("ctx", None, "head", None),
            P("ctx", None, "head", None),
            P(None, "ctx", "head", None),
            P(None, "ctx", "head", None),
            P("ctx"),
            P("head", "ctx"),
        ),
        out_specs=P(None, "head", "ctx"),
        check_vma=False,
    )
```

```python
import jax
import jax.numpy as jnp
from jax import lax
from jax.experimental import pallas as pl
from jax.experimental.pallas import tpu as pltpu
from jax.sharding import PartitionSpec as P

MESH = pl.DeviceIdType.MESH
F32, BF16 = jnp.float32, jnp.bfloat16
Z, QUAD, HEADS = 16, 4, 8
WINDOW = 4
BLOCK = 16
HD = 128
LOG2E = 1.4426950408889634
FAR_FIRST = sorted(range(1, Z), key=lambda d: -min(d, Z - d))


def nt(a, b):
    return lax.dot_general(a, b, (((1,), (1,)), ((), ())), preferred_element_type=F32)


def nn(a, b):
    return jnp.dot(a, b, preferred_element_type=F32)


def split2(x):
    high = x.astype(BF16)
    return high, (x - high.astype(F32)).astype(BF16)


def split3(x):
    high = x.astype(BF16)
    rest = x - high.astype(F32)
    middle = rest.astype(BF16)
    return high, middle, (rest - middle.astype(F32)).astype(BF16)


def kernel(
    q_in, k_in, v_in, sk_in, sv_in, nk_in, nv_in, len_in, w_in, out_ref,
    qbuf, kv, w, sk, sv, nk, nv, length, ka, kb, kc, vv, wh, wl,
    osend, orecv, lsend, lrecv, att, psend, precv,
    in_sem, a_send, a_recv, x_send, x_recv, o_send, o_recv, l_send, l_recv, c_send, c_recv, d_send, d_recv,
):
    ctx, head = lax.axis_index("ctx"), lax.axis_index("head")
    z, q = ctx // QUAD, lax.rem(ctx, QUAD)
    core, side = lax.rem(q, 2), q // 2
    x, y = lax.rem(head, 4), head // 4

    def along(d):
        return (lax.rem(ctx + QUAD * (d % Z), Z * QUAD), head)

    def head_of(d):
        return (1 - y if d & 4 else y) * 4 + lax.rem(x + (d & 3), 4)

    def in_quad(k, d=0):
        c = 1 - core if k & 1 else core
        s = 1 - side if k & 2 else side
        return (z * QUAD + s * 2 + c, head_of(d))

    def remote(src, dst, send, recv, to):
        return pltpu.make_async_remote_copy(
            src_ref=src, dst_ref=dst, send_sem=send, recv_sem=recv, device_id=to, device_id_type=MESH
        )

    window = [d for d in FAR_FIRST if min(d, Z - d) <= WINDOW]
    barrier = pltpu.get_barrier_semaphore()
    for d in window:
        pl.semaphore_signal(barrier, inc=1, device_id=along(d), device_id_type=MESH)
    greeted = [(0, 6), (0, 5), (0, 7), (0, 4), (0, 2), (0, 1), (0, 3), (2, 0), (3, 0), (1, 0)]
    for k, d in greeted:
        pl.semaphore_signal(barrier, inc=1, device_id=in_quad(k, d), device_id_type=MESH)
    mates = [(k, d) for d in (6, 5, 7, 4, 2, 1, 3, 0) for k in (2, 3, 1, 0) if (k, d) != (0, 0)]

    own = [
        pltpu.make_async_copy(src, dst, in_sem.at[i])
        for i, (src, dst) in enumerate(
            (
                (q_in, qbuf.at[0]), (k_in, kv.at[0, 0]), (v_in, kv.at[0, 1]), (sk_in, sk), (sv_in, sv),
                (nk_in, nk), (nv_in, nv), (len_in, length), (w_in, w.at[0]),
            )
        )
    ]
    for c in own:
        c.start()
    own[0].wait()
    own[1].wait()
    own[2].wait()
    pl.semaphore_wait(barrier, len(window) + len(greeted))

    first = {d: remote(qbuf.at[0], qbuf.at[Z - d], a_send.at[d], a_recv.at[d], along(d)) for d in window}
    for d in window:
        first[d].start()
    y_kv = [remote(kv.at[0, i], kv.at[2, i], x_send.at[i], x_recv.at[i], in_quad(2)) for i in (0, 1)]
    c_kv = [remote(kv.at[0, i], kv.at[1, i], x_send.at[2 + i], x_recv.at[2 + i], in_quad(1)) for i in (0, 1)]
    cy_kv = [remote(kv.at[2, i], kv.at[3, i], x_send.at[4 + i], x_recv.at[4 + i], in_quad(1)) for i in (0, 1)]
    y_w = remote(w.at[0], w.at[2], x_send.at[6], x_recv.at[6], in_quad(2))
    c_w = remote(w.at[0], w.at[1], x_send.at[7], x_recv.at[7], in_quad(1))
    cy_w = remote(w.at[2], w.at[3], x_send.at[8], x_recv.at[8], in_quad(1))
    for c in y_kv + c_kv:
        c.start()
    def prepare(i):
        rows = pl.ds(i * 256, 256)
        high, middle, low = split3(kv[i, 0])
        ka[rows, :] = jnp.concatenate([high, high], axis=1)
        kb[rows, :] = jnp.concatenate([middle, middle], axis=1)
        kc[rows, :] = jnp.concatenate([low, high], axis=1)
        high, low = split2(kv[i, 1])
        vv[rows, :] = jnp.concatenate([high, low], axis=1)

    prepare(0)
    second = []
    for k in range(1, WINDOW + 1):
        first[Z - k].wait_recv()
        c = remote(qbuf.at[k], qbuf.at[k + WINDOW], a_send.at[Z + k], a_recv.at[Z + k], along(-WINDOW))
        c.start()
        second.append(c)
        first[k].wait_recv()
        if k < WINDOW:
            c = remote(
                qbuf.at[Z - k], qbuf.at[Z - k - WINDOW], a_send.at[Z + 8 + k], a_recv.at[Z + 8 + k], along(WINDOW)
            )
            c.start()
            second.append(c)

    scale = HD**-0.5 * LOG2E
    sends = []

    def hand_out(d):
        sends.append(remote(osend.at[d], orecv.at[Z - d], o_send.at[d], o_recv.at[d], along(d)))
        sends.append(remote(lsend.at[d // 8], lrecv.at[Z - d], l_send.at[d], l_recv.at[d], along(d)))
        sends[-2].start()
        sends[-1].start()

    for c in c_kv:
        c.wait_recv()
    prepare(1)
    for i in (0, 1):
        y_kv[i].wait_recv()
        cy_kv[i].start()
    for c in own[3:]:
        c.wait()
    y_w.start()
    c_w.start()
    prepare(2)
    for c in second:
        c.wait_recv()
    high, middle, low = split3(qbuf[...].reshape(Z * BLOCK, HD) * scale)
    for c in cy_kv:
        c.wait_recv()
    prepare(3)
    first_two = jnp.concatenate([high, middle], axis=1)
    scores = nt(first_two, ka[...]) + nt(first_two, kb[...]) + nt(jnp.concatenate([high, low], axis=1), kc[...])
    peak = jnp.max(scores, axis=1, keepdims=True)
    weights = jnp.exp2(scores - peak)
    total = jnp.sum(weights, axis=1, keepdims=True)
    high, low = split2(weights)
    both = nn(high, vv[...]) + nn(low, vv[...])
    osend[...] = ((both[:, :HD] + both[:, HD:]) / total).reshape(Z, BLOCK, HD)
    lane = lax.broadcasted_iota(jnp.int32, (2, 128, 128), 2)
    row = lax.broadcasted_iota(jnp.int32, (2, 128, 128), 1)
    logs = (peak + jnp.log2(total)).reshape(2, 128, 1)
    lsend[...] = jnp.sum(jnp.where(lane == row, logs, 0.0), axis=1, keepdims=True)
    for d in FAR_FIRST:
        hand_out(d)

    queries = qbuf[0] * scale
    high, middle, low = split3(queries)
    kh, km, kl = split3(sk[...])
    scores = nt(high, kh) + nt(middle, kh) + nt(high, km) + nt(middle, km) + nt(high, kl) + nt(low, kh)
    lane16 = lax.broadcasted_iota(jnp.int32, (BLOCK, 128), 1)
    row16 = lax.broadcasted_iota(jnp.int32, (BLOCK, 128), 0)
    scores = jnp.where(lane16 < length[0], scores, -1e30)
    fresh = nk[...]
    new0 = jnp.sum(queries * fresh[0:1], axis=1, keepdims=True)
    new1 = jnp.sum(queries * fresh[1:2], axis=1, keepdims=True)
    new1 = jnp.where(row16[:, :1] >= 8, new1, -1e30)
    peak = jnp.maximum(jnp.max(scores, axis=1, keepdims=True), jnp.maximum(new0, new1))
    weights, new0, new1 = jnp.exp2(scores - peak), jnp.exp2(new0 - peak), jnp.exp2(new1 - peak)
    total = jnp.sum(weights, axis=1, keepdims=True) + new0 + new1
    wth, wtl = split2(weights)
    vh, vl = split2(sv[...])
    fresh = nv[...]
    mixed = nn(wth, vh) + nn(wth, vl) + nn(wtl, vh) + new0 * fresh[0:1] + new1 * fresh[1:2]
    parts = [(peak + jnp.log2(total), mixed / total)]

    def columns(k):
        high, low = split2(w[k])
        wh[k, 0:80] = high
        wl[k, 0:80] = low
        wh[k, 80:128] = jnp.zeros((48, 1024), BF16)
        wl[k, 80:128] = jnp.zeros((48, 1024), BF16)

    columns(0)
    c_w.wait_recv()
    columns(1)
    y_w.wait_recv()
    cy_w.start()
    columns(2)
    cy_w.wait_recv()
    columns(3)

    def logs_of(values, j):
        return jnp.sum(jnp.where(lane16 == row16 + BLOCK * j, values, 0.0), axis=1, keepdims=True)

    parts.append((logs_of(lsend[0], 0), osend[0]))
    for c in sends:
        c.wait_recv()
    for s in range(1, Z):
        mine = Z - s
        parts.append((logs_of(lrecv[s], mine % 8), orecv[s]))
    peak = parts[0][0]
    for logs, _ in parts[1:]:
        peak = jnp.maximum(peak, logs)
    total, mixed = jnp.zeros((BLOCK, 1), F32), jnp.zeros((BLOCK, HD), F32)
    for logs, value in parts:
        share = jnp.exp2(logs - peak)
        total += share
        mixed += share * value
    mine = pl.ds(pl.multiple_of(z * BLOCK, BLOCK), BLOCK)
    att[mine, :] = mixed / total

    spread = [remote(att.at[mine], att.at[mine], c_send.at[d], c_recv.at[d], along(d)) for d in FAR_FIRST]
    for c in spread:
        c.start()
    for c in spread:
        c.wait_recv()

    rows = jnp.concatenate([att[pl.ds(g, 32, stride=8), :] for g in range(8)], axis=1)
    high, low = split2(rows)
    halves = jnp.concatenate([high, low], axis=0)
    for k in range(QUAD):
        part = nt(halves, wh[k])
        part = part[:32] + part[32:] + nt(high, wl[k])
        for h in range(HEADS):
            psend[k, h] = part[4 * h : 4 * h + 4]
    last = []
    for k, d in mates:
        last.append(
            remote(
                psend.at[k, head_of(d)], precv.at[(d & 4) + (4 - (d & 3)) % 4, q],
                d_send.at[d * QUAD + k], d_recv.at[d * QUAD + k], in_quad(k, d),
            )
        )
        last[-1].start()
    precv[0, q] = psend[0, head]
    for c in last:
        c.wait_recv()
    summed = precv[0]
    for d in range(1, HEADS):
        summed += precv[d]
    for other in range(QUAD):
        for half in range(2):
            for t in range(2):
                out_ref[t, half * QUAD + other, :] = summed[other, half * 2 + t, :80]
    for c in list(first.values()) + second + y_kv + c_kv + cy_kv + [y_w, c_w, cy_w] + sends + spread + last:
        c.wait_send()


def local(
    queries, prompt_keys, prompt_values, suffix_keys, suffix_values, new_keys, new_values, suffix_lengths, out_weight
):
    dma = pltpu.SemaphoreType.DMA
    return pl.pallas_call(
        kernel,
        out_shape=pltpu.VMEM((2, 8, 80), F32),
        in_specs=[pl.BlockSpec(memory_space=pltpu.HBM)] * 9,
        out_specs=pl.BlockSpec(memory_space=pltpu.VMEM),
        scratch_shapes=[
            pltpu.VMEM((Z, BLOCK, HD), F32),
            pltpu.VMEM((QUAD, 2, 256, HD), F32),
            pltpu.VMEM((QUAD, 80, 1024), F32),
            pltpu.VMEM((128, HD), F32),
            pltpu.VMEM((128, HD), F32),
            pltpu.VMEM((2, HD), F32),
            pltpu.VMEM((2, HD), F32),
            pltpu.SMEM((1,), jnp.int32),
            pltpu.VMEM((1024, 256), BF16),
            pltpu.VMEM((1024, 256), BF16),
            pltpu.VMEM((1024, 256), BF16),
            pltpu.VMEM((1024, 256), BF16),
            pltpu.VMEM((QUAD, 128, 1024), BF16),
            pltpu.VMEM((QUAD, 128, 1024), BF16),
            pltpu.VMEM((Z, BLOCK, HD), F32),
            pltpu.VMEM((Z, BLOCK, HD), F32),
            pltpu.VMEM((2, 1, HD), F32),
            pltpu.VMEM((Z, 1, HD), F32),
            pltpu.VMEM((Z * BLOCK, HD), F32),
            pltpu.VMEM((QUAD, HEADS, 4, 128), F32),
            pltpu.VMEM((HEADS, QUAD, 4, 128), F32),
            dma((9,)),
            dma((28,)), dma((28,)),
            dma((9,)), dma((9,)),
            dma((Z,)), dma((Z,)),
            dma((Z,)), dma((Z,)),
            dma((Z,)), dma((Z,)),
            dma((HEADS * QUAD,)), dma((HEADS * QUAD,)),
        ],
        compiler_params=pltpu.CompilerParams(
            collective_id=0, has_side_effects=True, vmem_limit_bytes=60 * 2**20
        ),
    )(
        queries.reshape(BLOCK, HD),
        prompt_keys.reshape(256, HD),
        prompt_values.reshape(256, HD),
        suffix_keys.reshape(128, HD),
        suffix_values.reshape(128, HD),
        new_keys.reshape(2, HD),
        new_values.reshape(2, HD),
        suffix_lengths,
        out_weight.T,
    )


def solution(mesh):
    return jax.shard_map(
        local,
        mesh=mesh,
        in_specs=(
            P(None, "ctx", "head", None),
            P("ctx", "head", None),
            P("ctx", "head", None),
            P("ctx", None, "head", None),
            P("ctx", None, "head", None),
            P(None, "ctx", "head", None),
            P(None, "ctx", "head", None),
            P("ctx"),
            P("head", "ctx"),
        ),
        out_specs=P(None, "head", "ctx"),
        check_vma=False,
    )
```

```python
import jax
import jax.numpy as jnp
from jax import lax
from jax.experimental import pallas as pl
from jax.experimental.pallas import tpu as pltpu
from jax.sharding import PartitionSpec as P

MESH = pl.DeviceIdType.MESH
F32, BF16 = jnp.float32, jnp.bfloat16
Z, QUAD, HEADS = 16, 4, 8
WINDOW = 4
BLOCK = 16
HD = 128
LOG2E = 1.4426950408889634
FAR_FIRST = sorted(range(1, Z), key=lambda d: -min(d, Z - d))
(
    IN_Q, IN_KV, IN_SUF, IN_NEW, IN_LEN, IN_W, A_SEND, A_UP, A_DOWN, A_NEAR, A2_SEND, A2_RECV, KV_SEND, YK, YV, CKV,
    CYKV, W_SEND, YW, CW, CYW, B_SEND, B_RECV, C_SEND, C_RECV, D_SEND, D_RECV, SEMS,
) = range(28)


def nt(a, b):
    return lax.dot_general(a, b, (((1,), (1,)), ((), ())), preferred_element_type=F32)


def nn(a, b):
    return jnp.dot(a, b, preferred_element_type=F32)


def split2(x):
    high = x.astype(BF16)
    return high, (x - high.astype(F32)).astype(BF16)


def split3(x):
    high = x.astype(BF16)
    rest = x - high.astype(F32)
    middle = rest.astype(BF16)
    return high, middle, (rest - middle.astype(F32)).astype(BF16)


def kernel(
    q_in, k_in, v_in, sk_in, sv_in, nk_in, nv_in, len_in, w_in, out_ref,
    qbuf, kv, w, suf, new, length, ka, kb, kc, vv, wh, wl, osend, orecv, att, psend, precv, sem,
):
    ctx, head = lax.axis_index("ctx"), lax.axis_index("head")
    z, q = ctx // QUAD, lax.rem(ctx, QUAD)
    core, side = lax.rem(q, 2), q // 2
    x, y = lax.rem(head, 4), head // 4

    def along(d):
        return (lax.rem(ctx + QUAD * (d % Z), Z * QUAD), head)

    def head_of(d):
        return (1 - y if d & 4 else y) * 4 + lax.rem(x + (d & 3), 4)

    def in_quad(k, d=0):
        c = 1 - core if k & 1 else core
        s = 1 - side if k & 2 else side
        return (z * QUAD + s * 2 + c, head_of(d))

    def remote(src, dst, send, recv, to):
        return pltpu.make_async_remote_copy(
            src_ref=src, dst_ref=dst, send_sem=sem.at[send], recv_sem=sem.at[recv], device_id=to, device_id_type=MESH
        )

    def put(src, dst, send, recv, to):
        remote(src, dst, send, recv, to).start()

    def arrived(ref, recv):
        remote(ref, ref, recv, recv, in_quad(1)).wait_recv()

    def sent(ref, send):
        remote(ref, ref, send, send, in_quad(1)).wait_send()

    window = [d for d in FAR_FIRST if min(d, Z - d) <= WINDOW]
    barrier = pltpu.get_barrier_semaphore()
    for d in window:
        pl.semaphore_signal(barrier, inc=1, device_id=along(d), device_id_type=MESH)
    greeted = [(0, 6), (0, 5), (0, 7), (0, 4), (0, 2), (0, 1), (0, 3), (2, 0), (3, 0), (1, 0)]
    for k, d in greeted:
        pl.semaphore_signal(barrier, inc=1, device_id=in_quad(k, d), device_id_type=MESH)

    own = [
        pltpu.make_async_copy(src, dst, sem.at[i])
        for src, dst, i in (
            (q_in, qbuf.at[0], IN_Q), (k_in, kv.at[0, 0], IN_KV), (v_in, kv.at[0, 1], IN_KV),
            (sk_in, suf.at[0], IN_SUF), (sv_in, suf.at[1], IN_SUF), (nk_in, new.at[0], IN_NEW),
            (nv_in, new.at[1], IN_NEW), (len_in, length, IN_LEN), (w_in, w.at[0], IN_W),
        )
    ]
    for c in own:
        c.start()

    def loaded(ref, i):
        pltpu.make_async_copy(ref, ref, sem.at[i]).wait()

    loaded(qbuf.at[0], IN_Q)
    loaded(kv.at[0], IN_KV)
    pl.semaphore_wait(barrier, len(window) + len(greeted))

    for d in window:
        recv = A_UP if d == Z - WINDOW else A_DOWN if d == WINDOW else A_NEAR
        put(qbuf.at[0], qbuf.at[Z - d], A_SEND, recv, along(d))
    put(kv.at[0, 0], kv.at[2, 0], KV_SEND, YK, in_quad(2))
    put(kv.at[0, 1], kv.at[2, 1], KV_SEND, YV, in_quad(2))
    put(kv.at[0, 0], kv.at[1, 0], KV_SEND, CKV, in_quad(1))
    put(kv.at[0, 1], kv.at[1, 1], KV_SEND, CKV, in_quad(1))

    def prepare(i):
        rows = pl.ds(i * 256, 256)
        high, middle, low = split3(kv[i, 0])
        ka[rows, :] = jnp.concatenate([high, high], axis=1)
        kb[rows, :] = jnp.concatenate([middle, middle], axis=1)
        kc[rows, :] = jnp.concatenate([low, high], axis=1)
        high, low = split2(kv[i, 1])
        vv[rows, :] = jnp.concatenate([high, low], axis=1)

    prepare(0)
    for held, recv, hops in ((WINDOW, A_UP, (-4, -3, -2, -1)), (Z - WINDOW, A_DOWN, (3, 2, 1))):
        arrived(qbuf.at[held], recv)
        for d in hops:
            put(qbuf.at[held], qbuf.at[(held - d) % Z], A2_SEND, A2_RECV, along(d))
    arrived(qbuf.at[pl.ds(1, 6)], A_NEAR)

    arrived(kv.at[1], CKV)
    prepare(1)
    for i, recv in ((0, YK), (1, YV)):
        arrived(kv.at[2, i], recv)
        put(kv.at[2, i], kv.at[3, i], KV_SEND, CYKV, in_quad(1))
    loaded(w.at[0], IN_W)
    put(w.at[0], w.at[2], W_SEND, YW, in_quad(2))
    put(w.at[0], w.at[1], W_SEND, CW, in_quad(1))
    prepare(2)
    arrived(qbuf.at[pl.ds(5, 7)], A2_RECV)
    scale = HD**-0.5 * LOG2E
    high, middle, low = split3(qbuf[...].reshape(Z * BLOCK, HD) * scale)
    arrived(kv.at[3], CYKV)
    prepare(3)
    first_two = jnp.concatenate([high, middle], axis=1)
    scores = nt(first_two, ka[...]) + nt(first_two, kb[...]) + nt(jnp.concatenate([high, low], axis=1), kc[...])
    peak = jnp.max(scores, axis=1, keepdims=True)
    weights = jnp.exp2(scores - peak)
    total = jnp.sum(weights, axis=1, keepdims=True)
    high, low = split2(weights)
    both = nn(high, vv[...]) + nn(low, vv[...])
    osend[:, :BLOCK] = ((both[:, :HD] + both[:, HD:]) / total).reshape(Z, BLOCK, HD)
    lane = lax.broadcasted_iota(jnp.int32, (2, 128, 128), 2)
    row = lax.broadcasted_iota(jnp.int32, (2, 128, 128), 1)
    logs = (peak + jnp.log2(total)).reshape(2, 128, 1)
    logs = jnp.sum(jnp.where(lane == row, logs, 0.0), axis=1, keepdims=True)
    for d in range(Z):
        osend[d, BLOCK:] = logs[d // 8]
    for d in FAR_FIRST:
        put(osend.at[d], orecv.at[Z - d], B_SEND, B_RECV, along(d))

    loaded(suf, IN_SUF)
    loaded(new, IN_NEW)
    loaded(length, IN_LEN)
    queries = qbuf[0] * scale
    high, middle, low = split3(queries)
    kh, km, kl = split3(suf[0])
    scores = nt(high, kh) + nt(middle, kh) + nt(high, km) + nt(middle, km) + nt(high, kl) + nt(low, kh)
    lane16 = lax.broadcasted_iota(jnp.int32, (BLOCK, 128), 1)
    row16 = lax.broadcasted_iota(jnp.int32, (BLOCK, 128), 0)
    scores = jnp.where(lane16 < length[0], scores, -1e30)
    fresh = new[0]
    new0 = jnp.sum(queries * fresh[0:1], axis=1, keepdims=True)
    new1 = jnp.sum(queries * fresh[1:2], axis=1, keepdims=True)
    new1 = jnp.where(row16[:, :1] >= 8, new1, -1e30)
    peak = jnp.maximum(jnp.max(scores, axis=1, keepdims=True), jnp.maximum(new0, new1))
    weights, new0, new1 = jnp.exp2(scores - peak), jnp.exp2(new0 - peak), jnp.exp2(new1 - peak)
    total = jnp.sum(weights, axis=1, keepdims=True) + new0 + new1
    wth, wtl = split2(weights)
    vh, vl = split2(suf[1])
    fresh = new[1]
    mixed = nn(wth, vh) + nn(wth, vl) + nn(wtl, vh) + new0 * fresh[0:1] + new1 * fresh[1:2]
    parts = [(peak + jnp.log2(total), mixed / total)]

    def columns(k):
        high, low = split2(w[k])
        wh[k, 0:80] = high
        wl[k, 0:80] = low
        wh[k, 80:128] = jnp.zeros((48, 1024), BF16)
        wl[k, 80:128] = jnp.zeros((48, 1024), BF16)

    columns(0)
    arrived(w.at[1], CW)
    columns(1)
    arrived(w.at[2], YW)
    put(w.at[2], w.at[3], W_SEND, CYW, in_quad(1))
    columns(2)
    arrived(w.at[3], CYW)
    columns(3)
    sent(qbuf.at[pl.ds(0, 8)], A_SEND)
    sent(qbuf.at[pl.ds(0, 7)], A2_SEND)
    sent(kv.at[pl.ds(0, 3)], KV_SEND)
    sent(w.at[pl.ds(0, 3)], W_SEND)

    def logs_of(values, j):
        return jnp.sum(jnp.where(lane16 == row16 + BLOCK * j, values, 0.0), axis=1, keepdims=True)

    parts.append((logs_of(osend[0, BLOCK:], 0), osend[0, :BLOCK]))
    arrived(orecv.at[pl.ds(1, Z - 1)], B_RECV)
    for s in range(1, Z):
        mine = Z - s
        parts.append((logs_of(orecv[s, BLOCK:], mine % 8), orecv[s, :BLOCK]))
    peak = parts[0][0]
    for logs, _ in parts[1:]:
        peak = jnp.maximum(peak, logs)
    total, mixed = jnp.zeros((BLOCK, 1), F32), jnp.zeros((BLOCK, HD), F32)
    for logs, value in parts:
        share = jnp.exp2(logs - peak)
        total += share
        mixed += share * value
    mine = pl.ds(pl.multiple_of(z * BLOCK, BLOCK), BLOCK)
    att[mine, :] = mixed / total

    for d in FAR_FIRST:
        put(att.at[mine], att.at[mine], C_SEND, C_RECV, along(d))
    sent(osend.at[pl.ds(1, Z - 1)], B_SEND)
    arrived(att.at[pl.ds(0, (Z - 1) * BLOCK)], C_RECV)

    rows = jnp.concatenate([att[pl.ds(g, 32, stride=8), :] for g in range(8)], axis=1)
    high, low = split2(rows)
    halves = jnp.concatenate([high, low], axis=0)
    for k in (2, 3, 1, 0):
        part = nt(halves, wh[k])
        part = part[:32] + part[32:] + nt(high, wl[k])
        for h in range(HEADS):
            psend[k * HEADS + h] = part[4 * h : 4 * h + 4]
        for d in (6, 5, 7, 4, 2, 1, 3, 0):
            if (k, d) != (0, 0):
                slot = ((d & 4) + (4 - (d & 3)) % 4) * QUAD + q
                put(psend.at[k * HEADS + head_of(d)], precv.at[slot], D_SEND, D_RECV, in_quad(k, d))
    precv[q] = psend[head]
    sent(att.at[pl.ds(0, (Z - 1) * BLOCK)], C_SEND)
    sent(psend.at[pl.ds(0, HEADS * QUAD - 1)], D_SEND)
    arrived(precv.at[pl.ds(0, HEADS * QUAD - 1)], D_RECV)
    for other in range(QUAD):
        summed = precv[other]
        for d in range(1, HEADS):
            summed += precv[d * QUAD + other]
        for half in range(2):
            for t in range(2):
                out_ref[t, half * QUAD + other, :] = summed[half * 2 + t, :80]


def local(
    queries, prompt_keys, prompt_values, suffix_keys, suffix_values, new_keys, new_values, suffix_lengths, out_weight
):
    return pl.pallas_call(
        kernel,
        out_shape=pltpu.VMEM((2, 8, 80), F32),
        in_specs=[pl.BlockSpec(memory_space=pltpu.HBM)] * 9,
        out_specs=pl.BlockSpec(memory_space=pltpu.VMEM),
        scratch_shapes=[
            pltpu.VMEM((Z, BLOCK, HD), F32),
            pltpu.VMEM((QUAD, 2, 256, HD), F32),
            pltpu.VMEM((QUAD, 80, 1024), F32),
            pltpu.VMEM((2, 128, HD), F32),
            pltpu.VMEM((2, 2, HD), F32),
            pltpu.SMEM((1,), jnp.int32),
            pltpu.VMEM((1024, 256), BF16),
            pltpu.VMEM((1024, 256), BF16),
            pltpu.VMEM((1024, 256), BF16),
            pltpu.VMEM((1024, 256), BF16),
            pltpu.VMEM((QUAD, 128, 1024), BF16),
            pltpu.VMEM((QUAD, 128, 1024), BF16),
            pltpu.VMEM((Z, BLOCK + 1, HD), F32),
            pltpu.VMEM((Z, BLOCK + 1, HD), F32),
            pltpu.VMEM((Z * BLOCK, HD), F32),
            pltpu.VMEM((QUAD * HEADS, 4, 128), F32),
            pltpu.VMEM((HEADS * QUAD, 4, 128), F32),
            pltpu.SemaphoreType.DMA((SEMS,)),
        ],
        compiler_params=pltpu.CompilerParams(
            collective_id=0, has_side_effects=True, vmem_limit_bytes=60 * 2**20
        ),
    )(
        queries.reshape(BLOCK, HD),
        prompt_keys.reshape(256, HD),
        prompt_values.reshape(256, HD),
        suffix_keys.reshape(128, HD),
        suffix_values.reshape(128, HD),
        new_keys.reshape(2, HD),
        new_values.reshape(2, HD),
        suffix_lengths,
        out_weight.T,
    )


def solution(mesh):
    return jax.shard_map(
        local,
        mesh=mesh,
        in_specs=(
            P(None, "ctx", "head", None),
            P("ctx", "head", None),
            P("ctx", "head", None),
            P("ctx", None, "head", None),
            P("ctx", None, "head", None),
            P(None, "ctx", "head", None),
            P(None, "ctx", "head", None),
            P("ctx"),
            P("head", "ctx"),
        ),
        out_specs=P(None, "head", "ctx"),
        check_vma=False,
    )
```

```python
import jax
import jax.numpy as jnp
from jax import lax
from jax.experimental import pallas as pl
from jax.experimental.pallas import tpu as pltpu
from jax.sharding import PartitionSpec as P

MESH = pl.DeviceIdType.MESH
F32, BF16 = jnp.float32, jnp.bfloat16
Z, QUAD, HEADS = 16, 4, 8
WINDOW = 4
BLOCK = 16
HD = 128
LOG2E = 1.4426950408889634
FAR_FIRST = sorted(range(1, Z), key=lambda d: -min(d, Z - d))
(
    IN_Q, IN_KV, IN_SUF, IN_NEW, IN_LEN, IN_W, A_SEND, A_UP, A_DOWN, A_NEAR, A2_SEND, A2_RECV, KV_SEND, YK, YV, CKV,
    CYKV, W_SEND, YW, CW, CYW, B_SEND, B_RECV, C_SEND, C_RECV, D_SEND, D_RECV, SEMS,
) = range(28)


def nt(a, b):
    return lax.dot_general(a, b, (((1,), (1,)), ((), ())), preferred_element_type=F32)


def nn(a, b):
    return jnp.dot(a, b, preferred_element_type=F32)


def split2(x):
    high = x.astype(BF16)
    return high, (x - high.astype(F32)).astype(BF16)


def split3(x):
    high = x.astype(BF16)
    rest = x - high.astype(F32)
    middle = rest.astype(BF16)
    return high, middle, (rest - middle.astype(F32)).astype(BF16)


def kernel(
    q_in, k_in, v_in, sk_in, sv_in, nk_in, nv_in, len_in, w_in, out_ref,
    qbuf, kv, w, suf, new, length, ka, kb, kc, vv, wh, wl, osend, orecv, att, psend, precv, sem,
):
    ctx, head = lax.axis_index("ctx"), lax.axis_index("head")
    z, q = ctx // QUAD, lax.rem(ctx, QUAD)
    core, side = lax.rem(q, 2), q // 2
    x, y = lax.rem(head, 4), head // 4

    def along(d):
        return (lax.rem(ctx + QUAD * (d % Z), Z * QUAD), head)

    def head_of(d):
        return (1 - y if d & 4 else y) * 4 + lax.rem(x + (d & 3), 4)

    def in_quad(k, d=0):
        c = 1 - core if k & 1 else core
        s = 1 - side if k & 2 else side
        return (z * QUAD + s * 2 + c, head_of(d))

    def remote(src, dst, send, recv, to):
        return pltpu.make_async_remote_copy(
            src_ref=src, dst_ref=dst, send_sem=sem.at[send], recv_sem=sem.at[recv], device_id=to, device_id_type=MESH
        )

    def put(src, dst, send, recv, to):
        remote(src, dst, send, recv, to).start()

    def arrived(ref, recv):
        remote(ref, ref, recv, recv, in_quad(1)).wait_recv()

    def sent(ref, send):
        remote(ref, ref, send, send, in_quad(1)).wait_send()

    window = [d for d in FAR_FIRST if min(d, Z - d) <= WINDOW]
    barrier = pltpu.get_barrier_semaphore()
    for d in window:
        pl.semaphore_signal(barrier, inc=1, device_id=along(d), device_id_type=MESH)
    greeted = [(0, 6), (0, 5), (0, 7), (0, 4), (0, 2), (0, 1), (0, 3), (2, 0), (3, 0), (1, 0)]
    for k, d in greeted:
        pl.semaphore_signal(barrier, inc=1, device_id=in_quad(k, d), device_id_type=MESH)

    own = [
        pltpu.make_async_copy(src, dst, sem.at[i])
        for src, dst, i in (
            (q_in, qbuf.at[0], IN_Q), (k_in, kv.at[0, 0], IN_KV), (v_in, kv.at[0, 1], IN_KV),
            (sk_in, suf.at[0], IN_SUF), (sv_in, suf.at[1], IN_SUF), (nk_in, new.at[0], IN_NEW),
            (nv_in, new.at[1], IN_NEW), (len_in, length, IN_LEN), (w_in, w.at[0], IN_W),
        )
    ]
    for c in own:
        c.start()

    def loaded(ref, i):
        pltpu.make_async_copy(ref, ref, sem.at[i]).wait()

    loaded(qbuf.at[0], IN_Q)
    loaded(kv.at[0], IN_KV)
    pl.semaphore_wait(barrier, len(window) + len(greeted))

    for d in window:
        recv = A_UP if d == Z - WINDOW else A_DOWN if d == WINDOW else A_NEAR
        put(qbuf.at[0], qbuf.at[Z - d], A_SEND, recv, along(d))
    put(kv.at[0, 0], kv.at[2, 0], KV_SEND, YK, in_quad(2))
    put(kv.at[0, 1], kv.at[2, 1], KV_SEND, YV, in_quad(2))
    put(kv.at[0, 0], kv.at[1, 0], KV_SEND, CKV, in_quad(1))
    put(kv.at[0, 1], kv.at[1, 1], KV_SEND, CKV, in_quad(1))

    def prepare(i):
        rows = pl.ds(i * 256, 256)
        high, middle, low = split3(kv[i, 0])
        ka[rows, :] = jnp.concatenate([high, high], axis=1)
        kb[rows, :] = jnp.concatenate([middle, middle], axis=1)
        kc[rows, :] = jnp.concatenate([low, high], axis=1)
        high, low = split2(kv[i, 1])
        vv[rows, :] = jnp.concatenate([high, low], axis=1)

    prepare(0)
    for held, recv, hops in ((WINDOW, A_UP, (-4, -3, -2, -1)), (Z - WINDOW, A_DOWN, (3, 2, 1))):
        arrived(qbuf.at[held], recv)
        for d in hops:
            put(qbuf.at[held], qbuf.at[(held - d) % Z], A2_SEND, A2_RECV, along(d))
    arrived(qbuf.at[pl.ds(1, 6)], A_NEAR)

    arrived(kv.at[1], CKV)
    prepare(1)
    for i, recv in ((0, YK), (1, YV)):
        arrived(kv.at[2, i], recv)
        put(kv.at[2, i], kv.at[3, i], KV_SEND, CYKV, in_quad(1))
    loaded(w.at[0], IN_W)
    put(w.at[0], w.at[2], W_SEND, YW, in_quad(2))
    put(w.at[0], w.at[1], W_SEND, CW, in_quad(1))
    prepare(2)
    arrived(qbuf.at[pl.ds(5, 7)], A2_RECV)
    scale = HD**-0.5 * LOG2E
    high, middle, low = split3(qbuf[...].reshape(Z * BLOCK, HD) * scale)
    first_two = jnp.concatenate([high, middle], axis=1)
    first_last = jnp.concatenate([high, low], axis=1)

    def visit(start, size):
        rows = pl.ds(start, size)
        scores = nt(first_two, ka[rows, :]) + nt(first_two, kb[rows, :]) + nt(first_last, kc[rows, :])
        peak = jnp.max(scores, axis=1, keepdims=True)
        weights = jnp.exp2(scores - peak)
        total = jnp.sum(weights, axis=1, keepdims=True)
        high, low = split2(weights)
        both = nn(high, vv[rows, :]) + nn(low, vv[rows, :])
        return peak, total, both[:, :HD] + both[:, HD:]

    peak_a, total_a, mixed_a = visit(0, 768)
    arrived(kv.at[3], CYKV)
    prepare(3)
    peak_b, total_b, mixed_b = visit(768, 256)
    peak = jnp.maximum(peak_a, peak_b)
    share_a, share_b = jnp.exp2(peak_a - peak), jnp.exp2(peak_b - peak)
    total = total_a * share_a + total_b * share_b
    mixed = (mixed_a * share_a + mixed_b * share_b) / total
    osend[:, :BLOCK] = mixed.reshape(Z, BLOCK, HD)
    lane = lax.broadcasted_iota(jnp.int32, (2, 128, 128), 2)
    row = lax.broadcasted_iota(jnp.int32, (2, 128, 128), 1)
    logs = (peak + jnp.log2(total)).reshape(2, 128, 1)
    logs = jnp.sum(jnp.where(lane == row, logs, 0.0), axis=1, keepdims=True)
    for d in range(Z):
        osend[d, BLOCK:] = logs[d // 8]
    for d in FAR_FIRST:
        put(osend.at[d], orecv.at[Z - d], B_SEND, B_RECV, along(d))

    loaded(suf, IN_SUF)
    loaded(new, IN_NEW)
    loaded(length, IN_LEN)
    queries = qbuf[0] * scale
    high, middle, low = split3(queries)
    kh, km, kl = split3(suf[0])
    scores = nt(high, kh) + nt(middle, kh) + nt(high, km) + nt(middle, km) + nt(high, kl) + nt(low, kh)
    lane16 = lax.broadcasted_iota(jnp.int32, (BLOCK, 128), 1)
    row16 = lax.broadcasted_iota(jnp.int32, (BLOCK, 128), 0)
    scores = jnp.where(lane16 < length[0], scores, -1e30)
    fresh = new[0]
    new0 = jnp.sum(queries * fresh[0:1], axis=1, keepdims=True)
    new1 = jnp.sum(queries * fresh[1:2], axis=1, keepdims=True)
    new1 = jnp.where(row16[:, :1] >= 8, new1, -1e30)
    peak = jnp.maximum(jnp.max(scores, axis=1, keepdims=True), jnp.maximum(new0, new1))
    weights, new0, new1 = jnp.exp2(scores - peak), jnp.exp2(new0 - peak), jnp.exp2(new1 - peak)
    total = jnp.sum(weights, axis=1, keepdims=True) + new0 + new1
    wth, wtl = split2(weights)
    vh, vl = split2(suf[1])
    fresh = new[1]
    mixed = nn(wth, vh) + nn(wth, vl) + nn(wtl, vh) + new0 * fresh[0:1] + new1 * fresh[1:2]
    parts = [(peak + jnp.log2(total), mixed / total)]

    def columns(k):
        high, low = split2(w[k])
        wh[k, 0:80] = high
        wl[k, 0:80] = low
        wh[k, 80:128] = jnp.zeros((48, 1024), BF16)
        wl[k, 80:128] = jnp.zeros((48, 1024), BF16)

    columns(0)
    arrived(w.at[1], CW)
    columns(1)
    arrived(w.at[2], YW)
    put(w.at[2], w.at[3], W_SEND, CYW, in_quad(1))
    sent(qbuf.at[pl.ds(0, 8)], A_SEND)
    sent(qbuf.at[pl.ds(0, 7)], A2_SEND)
    sent(kv.at[pl.ds(0, 3)], KV_SEND)

    def logs_of(values, j):
        return jnp.sum(jnp.where(lane16 == row16 + BLOCK * j, values, 0.0), axis=1, keepdims=True)

    parts.append((logs_of(osend[0, BLOCK:], 0), osend[0, :BLOCK]))
    arrived(orecv.at[pl.ds(1, Z - 1)], B_RECV)
    for s in range(1, Z):
        mine = Z - s
        parts.append((logs_of(orecv[s, BLOCK:], mine % 8), orecv[s, :BLOCK]))
    peak = parts[0][0]
    for logs, _ in parts[1:]:
        peak = jnp.maximum(peak, logs)
    total, mixed = jnp.zeros((BLOCK, 1), F32), jnp.zeros((BLOCK, HD), F32)
    for logs, value in parts:
        share = jnp.exp2(logs - peak)
        total += share
        mixed += share * value
    mine = pl.ds(pl.multiple_of(z * BLOCK, BLOCK), BLOCK)
    att[mine, :] = mixed / total

    for d in FAR_FIRST:
        put(att.at[mine], att.at[mine], C_SEND, C_RECV, along(d))
    sent(osend.at[pl.ds(1, Z - 1)], B_SEND)
    columns(2)
    arrived(w.at[3], CYW)
    columns(3)
    sent(w.at[pl.ds(0, 3)], W_SEND)
    arrived(att.at[pl.ds(0, (Z - 1) * BLOCK)], C_RECV)

    rows = jnp.concatenate([att[pl.ds(g, 32, stride=8), :] for g in range(8)], axis=1)
    high, low = split2(rows)
    halves = jnp.concatenate([high, low], axis=0)
    for k in (2, 3, 1, 0):
        part = nt(halves, wh[k])
        part = part[:32] + part[32:] + nt(high, wl[k])
        for h in range(HEADS):
            psend[k * HEADS + h] = part[4 * h : 4 * h + 4]
        for d in (6, 5, 7, 4, 2, 1, 3, 0):
            if (k, d) != (0, 0):
                slot = ((d & 4) + (4 - (d & 3)) % 4) * QUAD + q
                put(psend.at[k * HEADS + head_of(d)], precv.at[slot], D_SEND, D_RECV, in_quad(k, d))
    precv[q] = psend[head]
    sent(att.at[pl.ds(0, (Z - 1) * BLOCK)], C_SEND)
    sent(psend.at[pl.ds(0, HEADS * QUAD - 1)], D_SEND)
    arrived(precv.at[pl.ds(0, HEADS * QUAD - 1)], D_RECV)
    for other in range(QUAD):
        summed = precv[other]
        for d in range(1, HEADS):
            summed += precv[d * QUAD + other]
        for half in range(2):
            for t in range(2):
                out_ref[t, half * QUAD + other, :] = summed[half * 2 + t, :80]


def local(
    queries, prompt_keys, prompt_values, suffix_keys, suffix_values, new_keys, new_values, suffix_lengths, out_weight
):
    return pl.pallas_call(
        kernel,
        out_shape=pltpu.VMEM((2, 8, 80), F32),
        in_specs=[pl.BlockSpec(memory_space=pltpu.HBM)] * 9,
        out_specs=pl.BlockSpec(memory_space=pltpu.VMEM),
        scratch_shapes=[
            pltpu.VMEM((Z, BLOCK, HD), F32),
            pltpu.VMEM((QUAD, 2, 256, HD), F32),
            pltpu.VMEM((QUAD, 80, 1024), F32),
            pltpu.VMEM((2, 128, HD), F32),
            pltpu.VMEM((2, 2, HD), F32),
            pltpu.SMEM((1,), jnp.int32),
            pltpu.VMEM((1024, 256), BF16),
            pltpu.VMEM((1024, 256), BF16),
            pltpu.VMEM((1024, 256), BF16),
            pltpu.VMEM((1024, 256), BF16),
            pltpu.VMEM((QUAD, 128, 1024), BF16),
            pltpu.VMEM((QUAD, 128, 1024), BF16),
            pltpu.VMEM((Z, BLOCK + 1, HD), F32),
            pltpu.VMEM((Z, BLOCK + 1, HD), F32),
            pltpu.VMEM((Z * BLOCK, HD), F32),
            pltpu.VMEM((QUAD * HEADS, 4, 128), F32),
            pltpu.VMEM((HEADS * QUAD, 4, 128), F32),
            pltpu.SemaphoreType.DMA((SEMS,)),
        ],
        compiler_params=pltpu.CompilerParams(
            collective_id=0, has_side_effects=True, vmem_limit_bytes=60 * 2**20
        ),
    )(
        queries.reshape(BLOCK, HD),
        prompt_keys.reshape(256, HD),
        prompt_values.reshape(256, HD),
        suffix_keys.reshape(128, HD),
        suffix_values.reshape(128, HD),
        new_keys.reshape(2, HD),
        new_values.reshape(2, HD),
        suffix_lengths,
        out_weight.T,
    )


def solution(mesh):
    return jax.shard_map(
        local,
        mesh=mesh,
        in_specs=(
            P(None, "ctx", "head", None),
            P("ctx", "head", None),
            P("ctx", "head", None),
            P("ctx", None, "head", None),
            P("ctx", None, "head", None),
            P(None, "ctx", "head", None),
            P(None, "ctx", "head", None),
            P("ctx"),
            P("head", "ctx"),
        ),
        out_specs=P(None, "head", "ctx"),
        check_vma=False,
    )
```

```python
import jax
import jax.numpy as jnp
from jax import lax
from jax.experimental import pallas as pl
from jax.experimental.pallas import tpu as pltpu
from jax.sharding import PartitionSpec as P

MESH = pl.DeviceIdType.MESH
F32, BF16 = jnp.float32, jnp.bfloat16
Z, QUAD, HEADS = 16, 4, 8
WINDOW = 4
BLOCK = 16
HD = 128
LOG2E = 1.4426950408889634
FAR_FIRST = sorted(range(1, Z), key=lambda d: -min(d, Z - d))
(
    IN_Q, IN_KV, IN_SUF, IN_NEW, IN_LEN, IN_W, A_SEND, A_UP, A_DOWN, A_NEAR, A2_SEND, A2_RECV, KV_SEND, YK, YV, CKV,
    CYK, CYV, W_SEND, YW, CW, CYW, B_SEND, B_RECV, C_SEND, C_RECV, D_SEND, D_RECV, SEMS,
) = range(29)


def nt(a, b):
    return lax.dot_general(a, b, (((1,), (1,)), ((), ())), preferred_element_type=F32)


def nn(a, b):
    return jnp.dot(a, b, preferred_element_type=F32)


def split2(x):
    high = x.astype(BF16)
    return high, (x - high.astype(F32)).astype(BF16)


def split3(x):
    high = x.astype(BF16)
    rest = x - high.astype(F32)
    middle = rest.astype(BF16)
    return high, middle, (rest - middle.astype(F32)).astype(BF16)


def kernel(
    q_in, k_in, v_in, sk_in, sv_in, nk_in, nv_in, len_in, w_in, out_ref,
    qbuf, kv, w, suf, new, length, ka, kb, kc, vv, wh, wl, osend, orecv, att, psend, precv, sem,
):
    ctx, head = lax.axis_index("ctx"), lax.axis_index("head")
    z, q = ctx // QUAD, lax.rem(ctx, QUAD)
    core, side = lax.rem(q, 2), q // 2
    x, y = lax.rem(head, 4), head // 4

    def along(d):
        return (lax.rem(ctx + QUAD * (d % Z), Z * QUAD), head)

    def head_of(d):
        return (1 - y if d & 4 else y) * 4 + lax.rem(x + (d & 3), 4)

    def in_quad(k, d=0):
        c = 1 - core if k & 1 else core
        s = 1 - side if k & 2 else side
        return (z * QUAD + s * 2 + c, head_of(d))

    def remote(src, dst, send, recv, to):
        return pltpu.make_async_remote_copy(
            src_ref=src, dst_ref=dst, send_sem=sem.at[send], recv_sem=sem.at[recv], device_id=to, device_id_type=MESH
        )

    def put(src, dst, send, recv, to):
        remote(src, dst, send, recv, to).start()

    def arrived(ref, recv):
        remote(ref, ref, recv, recv, in_quad(1)).wait_recv()

    def sent(ref, send):
        remote(ref, ref, send, send, in_quad(1)).wait_send()

    window = [d for d in FAR_FIRST if min(d, Z - d) <= WINDOW]
    barrier = pltpu.get_barrier_semaphore()
    for d in window:
        pl.semaphore_signal(barrier, inc=1, device_id=along(d), device_id_type=MESH)
    greeted = [(0, 6), (0, 5), (0, 7), (0, 4), (0, 2), (0, 1), (0, 3), (2, 0), (3, 0), (1, 0)]
    for k, d in greeted:
        pl.semaphore_signal(barrier, inc=1, device_id=in_quad(k, d), device_id_type=MESH)

    own = [
        pltpu.make_async_copy(src, dst, sem.at[i])
        for src, dst, i in (
            (q_in, qbuf.at[0], IN_Q), (k_in, kv.at[0, 0], IN_KV), (v_in, kv.at[0, 1], IN_KV),
            (sk_in, suf.at[0], IN_SUF), (sv_in, suf.at[1], IN_SUF), (nk_in, new.at[0], IN_NEW),
            (nv_in, new.at[1], IN_NEW), (len_in, length, IN_LEN), (w_in, w.at[0], IN_W),
        )
    ]
    for c in own:
        c.start()

    def loaded(ref, i):
        pltpu.make_async_copy(ref, ref, sem.at[i]).wait()

    loaded(qbuf.at[0], IN_Q)
    loaded(kv.at[0], IN_KV)
    pl.semaphore_wait(barrier, len(window) + len(greeted))

    put(kv.at[0, 0], kv.at[2, 0], KV_SEND, YK, in_quad(2))
    put(kv.at[0, 0], kv.at[1, 0], KV_SEND, CKV, in_quad(1))
    put(kv.at[0, 1], kv.at[2, 1], KV_SEND, YV, in_quad(2))
    put(kv.at[0, 1], kv.at[1, 1], KV_SEND, CKV, in_quad(1))

    for d in window:
        recv = A_UP if d == Z - WINDOW else A_DOWN if d == WINDOW else A_NEAR
        put(qbuf.at[0], qbuf.at[Z - d], A_SEND, recv, along(d))
    def prepare_keys(i):
        rows = pl.ds(i * 256, 256)
        high, middle, low = split3(kv[i, 0])
        ka[rows, :] = jnp.concatenate([high, high], axis=1)
        kb[rows, :] = jnp.concatenate([middle, middle], axis=1)
        kc[rows, :] = jnp.concatenate([low, high], axis=1)

    def prepare_values(i):
        high, low = split2(kv[i, 1])
        vv[pl.ds(i * 256, 256), :] = jnp.concatenate([high, low], axis=1)

    def prepare(i):
        prepare_keys(i)
        prepare_values(i)

    prepare(0)
    for held, recv, hops in ((WINDOW, A_UP, (-4, -3, -2, -1)), (Z - WINDOW, A_DOWN, (3, 2, 1))):
        arrived(qbuf.at[held], recv)
        for d in hops:
            put(qbuf.at[held], qbuf.at[(held - d) % Z], A2_SEND, A2_RECV, along(d))
    arrived(qbuf.at[pl.ds(1, 6)], A_NEAR)

    arrived(kv.at[1], CKV)
    prepare(1)
    for i, recv in ((0, YK), (1, YV)):
        arrived(kv.at[2, i], recv)
        put(kv.at[2, i], kv.at[3, i], KV_SEND, CYK + i, in_quad(1))
    loaded(w.at[0], IN_W)
    put(w.at[0], w.at[2], W_SEND, YW, in_quad(2))
    put(w.at[0], w.at[1], W_SEND, CW, in_quad(1))
    prepare(2)
    arrived(qbuf.at[pl.ds(5, 7)], A2_RECV)
    scale = HD**-0.5 * LOG2E
    high, middle, low = split3(qbuf[...].reshape(Z * BLOCK, HD) * scale)
    first_two = jnp.concatenate([high, middle], axis=1)
    first_last = jnp.concatenate([high, low], axis=1)

    def weigh(rows):
        scores = nt(first_two, ka[rows, :]) + nt(first_two, kb[rows, :]) + nt(first_last, kc[rows, :])
        peak = jnp.max(scores, axis=1, keepdims=True)
        weights = jnp.exp2(scores - peak)
        return peak, jnp.sum(weights, axis=1, keepdims=True), split2(weights)

    def mix(weights, rows):
        both = nn(weights[0], vv[rows, :]) + nn(weights[1], vv[rows, :])
        return both[:, :HD] + both[:, HD:]

    early, late = pl.ds(0, 768), pl.ds(768, 256)
    peak_a, total_a, weights = weigh(early)
    mixed_a = mix(weights, early)
    arrived(kv.at[3, 0], CYK)
    prepare_keys(3)
    peak_b, total_b, weights = weigh(late)
    peak = jnp.maximum(peak_a, peak_b)
    share_a, share_b = jnp.exp2(peak_a - peak), jnp.exp2(peak_b - peak)
    total = total_a * share_a + total_b * share_b
    mixed_a *= share_a / total
    share_b /= total
    lane = lax.broadcasted_iota(jnp.int32, (2, 128, 128), 2)
    row = lax.broadcasted_iota(jnp.int32, (2, 128, 128), 1)
    logs = (peak + jnp.log2(total)).reshape(2, 128, 1)
    logs = jnp.sum(jnp.where(lane == row, logs, 0.0), axis=1, keepdims=True)
    for d in range(Z):
        osend[d, BLOCK:] = logs[d // 8]
    arrived(kv.at[3, 1], CYV)
    prepare_values(3)
    mixed = mixed_a + mix(weights, late) * share_b
    osend[:, :BLOCK] = mixed.reshape(Z, BLOCK, HD)
    for d in FAR_FIRST:
        put(osend.at[d], orecv.at[Z - d], B_SEND, B_RECV, along(d))

    psend[...] = jnp.zeros_like(psend)
    loaded(suf, IN_SUF)
    loaded(new, IN_NEW)
    loaded(length, IN_LEN)
    queries = qbuf[0] * scale
    high, middle, low = split3(queries)
    kh, km, kl = split3(suf[0])
    scores = nt(high, kh) + nt(middle, kh) + nt(high, km) + nt(middle, km) + nt(high, kl) + nt(low, kh)
    lane16 = lax.broadcasted_iota(jnp.int32, (BLOCK, 128), 1)
    row16 = lax.broadcasted_iota(jnp.int32, (BLOCK, 128), 0)
    scores = jnp.where(lane16 < length[0], scores, -1e30)
    fresh = new[0]
    new0 = jnp.sum(queries * fresh[0:1], axis=1, keepdims=True)
    new1 = jnp.sum(queries * fresh[1:2], axis=1, keepdims=True)
    new1 = jnp.where(row16[:, :1] >= 8, new1, -1e30)
    peak = jnp.maximum(jnp.max(scores, axis=1, keepdims=True), jnp.maximum(new0, new1))
    weights, new0, new1 = jnp.exp2(scores - peak), jnp.exp2(new0 - peak), jnp.exp2(new1 - peak)
    total = jnp.sum(weights, axis=1, keepdims=True) + new0 + new1
    wth, wtl = split2(weights)
    vh, vl = split2(suf[1])
    fresh = new[1]
    mixed = nn(wth, vh) + nn(wth, vl) + nn(wtl, vh) + new0 * fresh[0:1] + new1 * fresh[1:2]
    parts = [(peak + jnp.log2(total), mixed / total)]

    def columns(k):
        wh[k], wl[k] = split2(w[k])

    columns(0)
    arrived(w.at[1], CW)
    columns(1)
    arrived(w.at[2], YW)
    put(w.at[2], w.at[3], W_SEND, CYW, in_quad(1))
    sent(qbuf.at[pl.ds(0, 8)], A_SEND)
    sent(qbuf.at[pl.ds(0, 7)], A2_SEND)
    sent(kv.at[pl.ds(0, 3)], KV_SEND)

    def logs_of(values, j):
        return jnp.sum(jnp.where(lane16 == row16 + BLOCK * j, values, 0.0), axis=1, keepdims=True)

    parts.append((logs_of(osend[0, BLOCK:], 0), osend[0, :BLOCK]))
    arrived(orecv.at[pl.ds(1, Z - 1)], B_RECV)
    for s in range(1, Z):
        mine = Z - s
        parts.append((logs_of(orecv[s, BLOCK:], mine % 8), orecv[s, :BLOCK]))
    peak = parts[0][0]
    for logs, _ in parts[1:]:
        peak = jnp.maximum(peak, logs)
    total, mixed = jnp.zeros((BLOCK, 1), F32), jnp.zeros((BLOCK, HD), F32)
    for logs, value in parts:
        share = jnp.exp2(logs - peak)
        total += share
        mixed += share * value
    mine = pl.ds(pl.multiple_of(z * BLOCK, BLOCK), BLOCK)
    att[mine, :] = mixed / total

    for d in FAR_FIRST:
        put(att.at[mine], att.at[mine], C_SEND, C_RECV, along(d))
    sent(osend.at[pl.ds(1, Z - 1)], B_SEND)
    columns(2)
    arrived(w.at[3], CYW)
    columns(3)
    sent(w.at[pl.ds(0, 3)], W_SEND)
    arrived(att.at[pl.ds(0, (Z - 1) * BLOCK)], C_RECV)

    rows = jnp.concatenate([att[pl.ds(g, 32, stride=8), :] for g in range(8)], axis=1)
    high, low = split2(rows)
    halves = jnp.concatenate([high, low], axis=0)
    for k in (2, 3, 1, 0):
        part = nt(halves, wh[k])
        part = part[:32] + part[32:] + nt(high, wl[k])
        for h in range(HEADS):
            psend[k * HEADS + h, :, :80] = part[4 * h : 4 * h + 4]
        for d in (6, 5, 7, 4, 2, 1, 3, 0):
            if (k, d) != (0, 0):
                slot = ((d & 4) + (4 - (d & 3)) % 4) * QUAD + q
                put(psend.at[k * HEADS + head_of(d)], precv.at[slot], D_SEND, D_RECV, in_quad(k, d))
    precv[q] = psend[head]
    sent(att.at[pl.ds(0, (Z - 1) * BLOCK)], C_SEND)
    sent(psend.at[pl.ds(0, HEADS * QUAD - 1)], D_SEND)
    arrived(precv.at[pl.ds(0, HEADS * QUAD - 1)], D_RECV)
    for other in range(QUAD):
        summed = precv[other]
        for d in range(1, HEADS):
            summed += precv[d * QUAD + other]
        for half in range(2):
            for t in range(2):
                out_ref[t, half * QUAD + other, :] = summed[half * 2 + t, :80]


def local(
    queries, prompt_keys, prompt_values, suffix_keys, suffix_values, new_keys, new_values, suffix_lengths, out_weight
):
    return pl.pallas_call(
        kernel,
        out_shape=pltpu.VMEM((2, 8, 80), F32),
        in_specs=[pl.BlockSpec(memory_space=pltpu.HBM)] * 9,
        out_specs=pl.BlockSpec(memory_space=pltpu.VMEM),
        scratch_shapes=[
            pltpu.VMEM((Z, BLOCK, HD), F32),
            pltpu.VMEM((QUAD, 2, 256, HD), F32),
            pltpu.VMEM((QUAD, 80, 1024), F32),
            pltpu.VMEM((2, 128, HD), F32),
            pltpu.VMEM((2, 2, HD), F32),
            pltpu.SMEM((1,), jnp.int32),
            pltpu.VMEM((1024, 256), BF16),
            pltpu.VMEM((1024, 256), BF16),
            pltpu.VMEM((1024, 256), BF16),
            pltpu.VMEM((1024, 256), BF16),
            pltpu.VMEM((QUAD, 80, 1024), BF16),
            pltpu.VMEM((QUAD, 80, 1024), BF16),
            pltpu.VMEM((Z, BLOCK + 1, HD), F32),
            pltpu.VMEM((Z, BLOCK + 1, HD), F32),
            pltpu.VMEM((Z * BLOCK, HD), F32),
            pltpu.VMEM((QUAD * HEADS, 4, 128), F32),
            pltpu.VMEM((HEADS * QUAD, 4, 128), F32),
            pltpu.SemaphoreType.DMA((SEMS,)),
        ],
        compiler_params=pltpu.CompilerParams(
            collective_id=0, has_side_effects=True, vmem_limit_bytes=60 * 2**20
        ),
    )(
        queries.reshape(BLOCK, HD),
        prompt_keys.reshape(256, HD),
        prompt_values.reshape(256, HD),
        suffix_keys.reshape(128, HD),
        suffix_values.reshape(128, HD),
        new_keys.reshape(2, HD),
        new_values.reshape(2, HD),
        suffix_lengths,
        out_weight.T,
    )


def solution(mesh):
    return jax.shard_map(
        local,
        mesh=mesh,
        in_specs=(
            P(None, "ctx", "head", None),
            P("ctx", "head", None),
            P("ctx", "head", None),
            P("ctx", None, "head", None),
            P("ctx", None, "head", None),
            P(None, "ctx", "head", None),
            P(None, "ctx", "head", None),
            P("ctx"),
            P("head", "ctx"),
        ),
        out_specs=P(None, "head", "ctx"),
        check_vma=False,
    )
```

```python
import jax
import jax.numpy as jnp
from jax import lax
from jax.experimental import pallas as pl
from jax.experimental.pallas import tpu as pltpu
from jax.sharding import PartitionSpec as P

MESH = pl.DeviceIdType.MESH
F32, BF16 = jnp.float32, jnp.bfloat16
Z, QUAD, HEADS = 16, 4, 8
WINDOW = 4
BLOCK = 16
HD = 128
LOG2E = 1.4426950408889634
FAR_FIRST = sorted(range(1, Z), key=lambda d: -min(d, Z - d))
(
    IN_Q, IN_KV, IN_SUF, IN_NEW, IN_LEN, IN_W, A_SEND, A_UP, A_DOWN, A_NEAR, A2_RECV, KV_SEND, YK, YV, CKV,
    CYK, CYV, W_SEND, YW, CW, CYW, B_SEND, B_RECV, C_SEND, C_RECV, D_SEND, D_RECV, SEMS,
) = range(28)


def nt(a, b):
    return lax.dot_general(a, b, (((1,), (1,)), ((), ())), preferred_element_type=F32)


def nn(a, b):
    return jnp.dot(a, b, preferred_element_type=F32)


def split2(x):
    high = x.astype(BF16)
    return high, (x - high.astype(F32)).astype(BF16)


def split3(x):
    high = x.astype(BF16)
    rest = x - high.astype(F32)
    middle = rest.astype(BF16)
    return high, middle, (rest - middle.astype(F32)).astype(BF16)


def kernel(
    q_in, k_in, v_in, sk_in, sv_in, nk_in, nv_in, len_in, w_in, out_ref,
    qbuf, kv, w, suf, new, length, ka, kb, kc, vv, wh, wl, osend, orecv, att, psend, precv, sem,
):
    ctx, head = lax.axis_index("ctx"), lax.axis_index("head")
    z, q = ctx // QUAD, lax.rem(ctx, QUAD)
    core, side = lax.rem(q, 2), q // 2
    x, y = lax.rem(head, 4), head // 4

    def along(d):
        return (lax.rem(ctx + QUAD * (d % Z), Z * QUAD), head)

    def head_of(d):
        return (1 - y if d & 4 else y) * 4 + lax.rem(x + (d & 3), 4)

    def in_quad(k, d=0):
        c = 1 - core if k & 1 else core
        s = 1 - side if k & 2 else side
        return (z * QUAD + s * 2 + c, head_of(d))

    def remote(src, dst, send, recv, to):
        return pltpu.make_async_remote_copy(
            src_ref=src, dst_ref=dst, send_sem=sem.at[send], recv_sem=sem.at[recv], device_id=to, device_id_type=MESH
        )

    def put(src, dst, send, recv, to):
        remote(src, dst, send, recv, to).start()

    def arrived(ref, recv):
        remote(ref, ref, recv, recv, in_quad(1)).wait_recv()

    def sent(ref, send):
        remote(ref, ref, send, send, in_quad(1)).wait_send()

    window = [d for d in FAR_FIRST if min(d, Z - d) <= WINDOW]
    barrier = pltpu.get_barrier_semaphore()
    for d in window:
        pl.semaphore_signal(barrier, inc=1, device_id=along(d), device_id_type=MESH)
    greeted = [(0, 6), (0, 5), (0, 7), (0, 4), (0, 2), (0, 1), (0, 3), (2, 0), (3, 0), (1, 0)]
    for k, d in greeted:
        pl.semaphore_signal(barrier, inc=1, device_id=in_quad(k, d), device_id_type=MESH)

    own = [
        pltpu.make_async_copy(src, dst, sem.at[i])
        for src, dst, i in (
            (q_in, qbuf.at[0], IN_Q), (k_in, kv.at[0, 0], IN_KV), (v_in, kv.at[0, 1], IN_KV),
            (sk_in, suf.at[0], IN_SUF), (sv_in, suf.at[1], IN_SUF), (nk_in, new.at[0], IN_NEW),
            (nv_in, new.at[1], IN_NEW), (len_in, length, IN_LEN), (w_in, w.at[0], IN_W),
        )
    ]
    for c in own[:3]:
        c.start()

    def loaded(ref, i):
        pltpu.make_async_copy(ref, ref, sem.at[i]).wait()

    loaded(qbuf.at[0], IN_Q)
    loaded(kv.at[0], IN_KV)
    pl.semaphore_wait(barrier, len(window) + len(greeted))

    put(kv.at[0, 0], kv.at[2, 0], KV_SEND, YK, in_quad(2))
    put(kv.at[0, 0], kv.at[1, 0], KV_SEND, CKV, in_quad(1))
    put(kv.at[0, 1], kv.at[2, 1], KV_SEND, YV, in_quad(2))
    put(kv.at[0, 1], kv.at[1, 1], KV_SEND, CKV, in_quad(1))

    for d in window:
        recv = A_UP if d == Z - WINDOW else A_DOWN if d == WINDOW else A_NEAR
        put(qbuf.at[0], qbuf.at[Z - d], A_SEND, recv, along(d))
    def prepare_keys(i):
        rows = pl.ds(i * 256, 256)
        high, middle, low = split3(kv[i, 0])
        ka[rows, :] = jnp.concatenate([high, high], axis=1)
        kb[rows, :] = jnp.concatenate([middle, middle], axis=1)
        kc[rows, :] = jnp.concatenate([low, high], axis=1)

    def prepare_values(i):
        high, low = split2(kv[i, 1])
        vv[pl.ds(i * 256, 256), :] = jnp.concatenate([high, low], axis=1)

    def prepare(i):
        prepare_keys(i)
        prepare_values(i)

    for c in own[3:]:
        c.start()
    prepare(0)
    for held, recv, hops in ((WINDOW, A_UP, (-4, -3, -2, -1)), (Z - WINDOW, A_DOWN, (3, 2, 1))):
        arrived(qbuf.at[held], recv)
        for d in hops:
            put(qbuf.at[held], qbuf.at[(held - d) % Z], A_SEND, A2_RECV, along(d))
    arrived(qbuf.at[pl.ds(1, 6)], A_NEAR)

    arrived(kv.at[1], CKV)
    prepare(1)
    for i, recv in ((0, YK), (1, YV)):
        arrived(kv.at[2, i], recv)
        put(kv.at[2, i], kv.at[3, i], KV_SEND, CYK + i, in_quad(1))
    loaded(w.at[0], IN_W)
    put(w.at[0], w.at[2], W_SEND, YW, in_quad(2))
    put(w.at[0], w.at[1], W_SEND, CW, in_quad(1))
    prepare(2)
    arrived(qbuf.at[pl.ds(5, 7)], A2_RECV)
    scale = HD**-0.5 * LOG2E
    high, middle, low = split3(qbuf[...].reshape(Z * BLOCK, HD) * scale)
    first_two = jnp.concatenate([high, middle], axis=1)
    first_last = jnp.concatenate([high, low], axis=1)

    def weigh(rows):
        scores = nt(first_two, ka[rows, :]) + nt(first_two, kb[rows, :]) + nt(first_last, kc[rows, :])
        peak = jnp.max(scores, axis=1, keepdims=True)
        weights = jnp.exp2(scores - peak)
        return peak, jnp.sum(weights, axis=1, keepdims=True), split2(weights)

    def mix(weights, rows):
        both = nn(weights[0], vv[rows, :]) + nn(weights[1], vv[rows, :])
        return both[:, :HD] + both[:, HD:]

    early, late = pl.ds(0, 768), pl.ds(768, 256)
    peak_a, total_a, weights = weigh(early)
    mixed_a = mix(weights, early)
    arrived(kv.at[3, 0], CYK)
    prepare_keys(3)
    peak_b, total_b, weights = weigh(late)
    peak = jnp.maximum(peak_a, peak_b)
    share_a, share_b = jnp.exp2(peak_a - peak), jnp.exp2(peak_b - peak)
    total = total_a * share_a + total_b * share_b
    mixed_a *= share_a / total
    share_b /= total
    lane = lax.broadcasted_iota(jnp.int32, (2, 128, 128), 2)
    row = lax.broadcasted_iota(jnp.int32, (2, 128, 128), 1)
    logs = (peak + jnp.log2(total)).reshape(2, 128, 1)
    logs = jnp.sum(jnp.where(lane == row, logs, 0.0), axis=1, keepdims=True)
    for d in range(Z):
        osend[d, BLOCK:] = logs[d // 8]
    arrived(kv.at[3, 1], CYV)
    prepare_values(3)
    mixed = mixed_a + mix(weights, late) * share_b
    osend[:, :BLOCK] = mixed.reshape(Z, BLOCK, HD)
    for d in FAR_FIRST:
        put(osend.at[d], orecv.at[Z - d], B_SEND, B_RECV, along(d))

    psend[...] = jnp.zeros_like(psend)
    loaded(suf, IN_SUF)
    loaded(new, IN_NEW)
    loaded(length, IN_LEN)
    queries = qbuf[0] * scale
    high, middle, low = split3(queries)
    kh, km, kl = split3(suf[0])
    scores = nt(high, kh) + nt(middle, kh) + nt(high, km) + nt(middle, km) + nt(high, kl) + nt(low, kh)
    lane16 = lax.broadcasted_iota(jnp.int32, (BLOCK, 128), 1)
    row16 = lax.broadcasted_iota(jnp.int32, (BLOCK, 128), 0)
    scores = jnp.where(lane16 < length[0], scores, -1e30)
    fresh = new[0]
    new0 = jnp.sum(queries * fresh[0:1], axis=1, keepdims=True)
    new1 = jnp.sum(queries * fresh[1:2], axis=1, keepdims=True)
    new1 = jnp.where(row16[:, :1] >= 8, new1, -1e30)
    peak = jnp.maximum(jnp.max(scores, axis=1, keepdims=True), jnp.maximum(new0, new1))
    weights, new0, new1 = jnp.exp2(scores - peak), jnp.exp2(new0 - peak), jnp.exp2(new1 - peak)
    total = jnp.sum(weights, axis=1, keepdims=True) + new0 + new1
    wth, wtl = split2(weights)
    vh, vl = split2(suf[1])
    fresh = new[1]
    mixed = nn(wth, vh) + nn(wth, vl) + nn(wtl, vh) + new0 * fresh[0:1] + new1 * fresh[1:2]
    parts = [(peak + jnp.log2(total), mixed / total)]

    def columns(k):
        wh[k], wl[k] = split2(w[k])

    columns(0)
    arrived(w.at[1], CW)
    columns(1)
    arrived(w.at[2], YW)
    put(w.at[2], w.at[3], W_SEND, CYW, in_quad(1))
    sent(qbuf.at[pl.ds(0, 15)], A_SEND)
    sent(kv.at[pl.ds(0, 3)], KV_SEND)

    def logs_of(values, j):
        return jnp.sum(jnp.where(lane16 == row16 + BLOCK * j, values, 0.0), axis=1, keepdims=True)

    parts.append((logs_of(osend[0, BLOCK:], 0), osend[0, :BLOCK]))
    arrived(orecv.at[pl.ds(1, Z - 1)], B_RECV)
    for s in range(1, Z):
        mine = Z - s
        parts.append((logs_of(orecv[s, BLOCK:], mine % 8), orecv[s, :BLOCK]))
    peak = parts[0][0]
    for logs, _ in parts[1:]:
        peak = jnp.maximum(peak, logs)
    total, mixed = jnp.zeros((BLOCK, 1), F32), jnp.zeros((BLOCK, HD), F32)
    for logs, value in parts:
        share = jnp.exp2(logs - peak)
        total += share
        mixed += share * value
    mine = pl.ds(pl.multiple_of(z * BLOCK, BLOCK), BLOCK)
    att[mine, :] = mixed / total

    for d in FAR_FIRST:
        put(att.at[mine], att.at[mine], C_SEND, C_RECV, along(d))
    sent(osend.at[pl.ds(1, Z - 1)], B_SEND)
    columns(2)
    arrived(w.at[3], CYW)
    columns(3)
    sent(w.at[pl.ds(0, 3)], W_SEND)
    arrived(att.at[pl.ds(0, (Z - 1) * BLOCK)], C_RECV)

    rows = jnp.concatenate([att[pl.ds(g, 32, stride=8), :] for g in range(8)], axis=1)
    high, low = split2(rows)
    halves = jnp.concatenate([high, low], axis=0)
    for k in (2, 3, 1, 0):
        part = nt(halves, wh[k])
        part = part[:32] + part[32:] + nt(high, wl[k])
        for h in range(HEADS):
            psend[k * HEADS + h, :, :80] = part[4 * h : 4 * h + 4]
        for d in (6, 5, 7, 4, 2, 1, 3, 0):
            if (k, d) != (0, 0):
                slot = ((d & 4) + (4 - (d & 3)) % 4) * QUAD + q
                put(psend.at[k * HEADS + head_of(d)], precv.at[slot], D_SEND, D_RECV, in_quad(k, d))
    precv[q] = psend[head]
    sent(att.at[pl.ds(0, (Z - 1) * BLOCK)], C_SEND)
    sent(psend.at[pl.ds(0, HEADS * QUAD - 1)], D_SEND)
    arrived(precv.at[pl.ds(0, HEADS * QUAD - 1)], D_RECV)
    for other in range(QUAD):
        summed = precv[other]
        for d in range(1, HEADS):
            summed += precv[d * QUAD + other]
        for half in range(2):
            for t in range(2):
                out_ref[t, half * QUAD + other, :] = summed[half * 2 + t, :80]


def local(
    queries, prompt_keys, prompt_values, suffix_keys, suffix_values, new_keys, new_values, suffix_lengths, out_weight
):
    return pl.pallas_call(
        kernel,
        out_shape=pltpu.VMEM((2, 8, 80), F32),
        in_specs=[pl.BlockSpec(memory_space=pltpu.HBM)] * 9,
        out_specs=pl.BlockSpec(memory_space=pltpu.VMEM),
        scratch_shapes=[
            pltpu.VMEM((Z, BLOCK, HD), F32),
            pltpu.VMEM((QUAD, 2, 256, HD), F32),
            pltpu.VMEM((QUAD, 80, 1024), F32),
            pltpu.VMEM((2, 128, HD), F32),
            pltpu.VMEM((2, 2, HD), F32),
            pltpu.SMEM((1,), jnp.int32),
            pltpu.VMEM((1024, 256), BF16),
            pltpu.VMEM((1024, 256), BF16),
            pltpu.VMEM((1024, 256), BF16),
            pltpu.VMEM((1024, 256), BF16),
            pltpu.VMEM((QUAD, 80, 1024), BF16),
            pltpu.VMEM((QUAD, 80, 1024), BF16),
            pltpu.VMEM((Z, BLOCK + 1, HD), F32),
            pltpu.VMEM((Z, BLOCK + 1, HD), F32),
            pltpu.VMEM((Z * BLOCK, HD), F32),
            pltpu.VMEM((QUAD * HEADS, 4, 128), F32),
            pltpu.VMEM((HEADS * QUAD, 4, 128), F32),
            pltpu.SemaphoreType.DMA((SEMS,)),
        ],
        compiler_params=pltpu.CompilerParams(
            collective_id=0, has_side_effects=True, vmem_limit_bytes=60 * 2**20
        ),
    )(
        queries.reshape(BLOCK, HD),
        prompt_keys.reshape(256, HD),
        prompt_values.reshape(256, HD),
        suffix_keys.reshape(128, HD),
        suffix_values.reshape(128, HD),
        new_keys.reshape(2, HD),
        new_values.reshape(2, HD),
        suffix_lengths,
        out_weight.T,
    )


def solution(mesh):
    return jax.shard_map(
        local,
        mesh=mesh,
        in_specs=(
            P(None, "ctx", "head", None),
            P("ctx", "head", None),
            P("ctx", "head", None),
            P("ctx", None, "head", None),
            P("ctx", None, "head", None),
            P(None, "ctx", "head", None),
            P(None, "ctx", "head", None),
            P("ctx"),
            P("head", "ctx"),
        ),
        out_specs=P(None, "head", "ctx"),
        check_vma=False,
    )
```

```python
import jax
import jax.numpy as jnp
from jax import lax
from jax.experimental import pallas as pl
from jax.experimental.pallas import tpu as pltpu
from jax.sharding import PartitionSpec as P

MESH = pl.DeviceIdType.MESH
F32, BF16 = jnp.float32, jnp.bfloat16
Z, QUAD, HEADS = 16, 4, 8
WINDOW = 4
BLOCK = 16
HD = 128
LOG2E = 1.4426950408889634
FAR_FIRST = sorted(range(1, Z), key=lambda d: -min(d, Z - d))
(
    IN_Q, IN_KV, IN_SUF, IN_NEW, IN_LEN, IN_W, A_SEND, A_UP, A_DOWN, A_NEAR, A2_SEND, A2_RECV, KV_SEND, YK, YV, CKV,
    CYK, CYV, W_SEND, YW, CW, CYW, B_SEND, B_RECV, C_SEND, C_RECV, D_SEND, D_RECV, SEMS,
) = range(29)


def nt(a, b):
    return lax.dot_general(a, b, (((1,), (1,)), ((), ())), preferred_element_type=F32)


def nn(a, b):
    return jnp.dot(a, b, preferred_element_type=F32)


def split2(x):
    high = x.astype(BF16)
    return high, (x - high.astype(F32)).astype(BF16)


def split3(x):
    high = x.astype(BF16)
    rest = x - high.astype(F32)
    middle = rest.astype(BF16)
    return high, middle, (rest - middle.astype(F32)).astype(BF16)


def kernel(
    q_in, k_in, v_in, sk_in, sv_in, nk_in, nv_in, len_in, w_in, out_ref,
    qbuf, kv, w, suf, new, length, ka, kb, kc, vv, wh, wl, osend, orecv, att, psend, precv, sem,
):
    ctx, head = lax.axis_index("ctx"), lax.axis_index("head")
    z, q = ctx // QUAD, lax.rem(ctx, QUAD)
    core, side = lax.rem(q, 2), q // 2
    x, y = lax.rem(head, 4), head // 4

    def along(d):
        return (lax.rem(ctx + QUAD * (d % Z), Z * QUAD), head)

    def head_of(d):
        return (1 - y if d & 4 else y) * 4 + lax.rem(x + (d & 3), 4)

    def in_quad(k, d=0):
        c = 1 - core if k & 1 else core
        s = 1 - side if k & 2 else side
        return (z * QUAD + s * 2 + c, head_of(d))

    def remote(src, dst, send, recv, to):
        return pltpu.make_async_remote_copy(
            src_ref=src, dst_ref=dst, send_sem=sem.at[send], recv_sem=sem.at[recv], device_id=to, device_id_type=MESH
        )

    def put(src, dst, send, recv, to):
        remote(src, dst, send, recv, to).start()

    def arrived(ref, recv):
        remote(ref, ref, recv, recv, in_quad(1)).wait_recv()

    def sent(ref, send):
        remote(ref, ref, send, send, in_quad(1)).wait_send()

    window = [d for d in FAR_FIRST if min(d, Z - d) <= WINDOW]
    barrier = pltpu.get_barrier_semaphore()
    for d in window:
        pl.semaphore_signal(barrier, inc=1, device_id=along(d), device_id_type=MESH)
    greeted = [(0, 6), (0, 5), (0, 7), (0, 4), (0, 2), (0, 1), (0, 3), (2, 0), (3, 0), (1, 0)]
    for k, d in greeted:
        pl.semaphore_signal(barrier, inc=1, device_id=in_quad(k, d), device_id_type=MESH)

    own = [
        pltpu.make_async_copy(src, dst, sem.at[i])
        for src, dst, i in (
            (q_in, qbuf.at[0], IN_Q), (k_in, kv.at[0, 0], IN_KV), (v_in, kv.at[0, 1], IN_KV),
            (sk_in, suf.at[0], IN_SUF), (sv_in, suf.at[1], IN_SUF), (nk_in, new.at[0], IN_NEW),
            (nv_in, new.at[1], IN_NEW), (len_in, length, IN_LEN), (w_in, w.at[0], IN_W),
        )
    ]
    for c in own:
        c.start()

    def loaded(ref, i):
        pltpu.make_async_copy(ref, ref, sem.at[i]).wait()

    loaded(qbuf.at[0], IN_Q)
    loaded(kv.at[0], IN_KV)
    pl.semaphore_wait(barrier, len(window) + len(greeted))

    put(kv.at[0, 0], kv.at[2, 0], KV_SEND, YK, in_quad(2))
    put(kv.at[0, 0], kv.at[1, 0], KV_SEND, CKV, in_quad(1))
    put(kv.at[0, 1], kv.at[2, 1], KV_SEND, YV, in_quad(2))
    put(kv.at[0, 1], kv.at[1, 1], KV_SEND, CKV, in_quad(1))

    for d in window:
        recv = A_UP if d == Z - WINDOW else A_DOWN if d == WINDOW else A_NEAR
        put(qbuf.at[0], qbuf.at[Z - d], A_SEND, recv, along(d))
    def prepare_keys(i):
        rows = pl.ds(i * 256, 256)
        high, middle, low = split3(kv[i, 0])
        ka[rows, :] = jnp.concatenate([high, high], axis=1)
        kb[rows, :] = jnp.concatenate([middle, middle], axis=1)
        kc[rows, :] = jnp.concatenate([low, high], axis=1)

    def prepare_values(i):
        high, low = split2(kv[i, 1])
        vv[pl.ds(i * 256, 256), :] = jnp.concatenate([high, low], axis=1)

    def prepare(i):
        prepare_keys(i)
        prepare_values(i)

    prepare(0)
    for held, recv, hops in ((WINDOW, A_UP, (-4, -3, -2, -1)), (Z - WINDOW, A_DOWN, (3, 2, 1))):
        arrived(qbuf.at[held], recv)
        for d in hops:
            put(qbuf.at[held], qbuf.at[(held - d) % Z], A2_SEND, A2_RECV, along(d))
    arrived(qbuf.at[pl.ds(1, 6)], A_NEAR)

    arrived(kv.at[1], CKV)
    prepare(1)
    for i, recv in ((0, YK), (1, YV)):
        arrived(kv.at[2, i], recv)
        put(kv.at[2, i], kv.at[3, i], KV_SEND, CYK + i, in_quad(1))
    loaded(w.at[0], IN_W)
    put(w.at[0], w.at[2], W_SEND, YW, in_quad(2))
    put(w.at[0], w.at[1], W_SEND, CW, in_quad(1))
    prepare(2)
    arrived(qbuf.at[pl.ds(5, 7)], A2_RECV)
    scale = HD**-0.5 * LOG2E
    high, middle, low = split3(qbuf[...].reshape(Z * BLOCK, HD) * scale)
    first_two = jnp.concatenate([high, middle], axis=1)
    first_last = jnp.concatenate([high, low], axis=1)

    def weigh(rows):
        scores = nt(first_two, ka[rows, :]) + nt(first_two, kb[rows, :]) + nt(first_last, kc[rows, :])
        peak = jnp.max(scores, axis=1, keepdims=True)
        weights = jnp.exp2(scores - peak)
        return peak, jnp.sum(weights, axis=1, keepdims=True), split2(weights)

    def mix(weights, rows):
        both = nn(weights[0], vv[rows, :]) + nn(weights[1], vv[rows, :])
        return both[:, :HD] + both[:, HD:]

    early, late = pl.ds(0, 768), pl.ds(768, 256)
    peak_a, total_a, weights = weigh(early)
    mixed_a = mix(weights, early)
    arrived(kv.at[3, 0], CYK)
    prepare_keys(3)
    peak_b, total_b, weights = weigh(late)
    peak = jnp.maximum(peak_a, peak_b)
    share_a, share_b = jnp.exp2(peak_a - peak), jnp.exp2(peak_b - peak)
    total = total_a * share_a + total_b * share_b
    mixed_a *= share_a / total
    share_b /= total
    lane = lax.broadcasted_iota(jnp.int32, (2, 128, 128), 2)
    row = lax.broadcasted_iota(jnp.int32, (2, 128, 128), 1)
    logs = (peak + jnp.log2(total)).reshape(2, 128, 1)
    logs = jnp.sum(jnp.where(lane == row, logs, 0.0), axis=1, keepdims=True)
    for d in range(Z):
        osend[d, BLOCK:] = logs[d // 8]
    arrived(kv.at[3, 1], CYV)
    prepare_values(3)

    def hand_out(first, last):
        rows = slice(first * BLOCK, last * BLOCK)
        mixed = mixed_a[rows] + mix([w[rows] for w in weights], late) * share_b[rows]
        osend[first:last, :BLOCK] = mixed.reshape(last - first, BLOCK, HD)
        for d in FAR_FIRST:
            if first <= d < last:
                put(osend.at[d], orecv.at[Z - d], B_SEND, B_RECV, along(d))

    hand_out(4, 12)
    hand_out(12, 16)
    hand_out(0, 4)

    psend[...] = jnp.zeros_like(psend)
    loaded(suf, IN_SUF)
    loaded(new, IN_NEW)
    loaded(length, IN_LEN)
    queries = qbuf[0] * scale
    high, middle, low = split3(queries)
    kh, km, kl = split3(suf[0])
    scores = nt(high, kh) + nt(middle, kh) + nt(high, km) + nt(middle, km) + nt(high, kl) + nt(low, kh)
    lane16 = lax.broadcasted_iota(jnp.int32, (BLOCK, 128), 1)
    row16 = lax.broadcasted_iota(jnp.int32, (BLOCK, 128), 0)
    scores = jnp.where(lane16 < length[0], scores, -1e30)
    fresh = new[0]
    new0 = jnp.sum(queries * fresh[0:1], axis=1, keepdims=True)
    new1 = jnp.sum(queries * fresh[1:2], axis=1, keepdims=True)
    new1 = jnp.where(row16[:, :1] >= 8, new1, -1e30)
    peak = jnp.maximum(jnp.max(scores, axis=1, keepdims=True), jnp.maximum(new0, new1))
    weights, new0, new1 = jnp.exp2(scores - peak), jnp.exp2(new0 - peak), jnp.exp2(new1 - peak)
    total = jnp.sum(weights, axis=1, keepdims=True) + new0 + new1
    wth, wtl = split2(weights)
    vh, vl = split2(suf[1])
    fresh = new[1]
    mixed = nn(wth, vh) + nn(wth, vl) + nn(wtl, vh) + new0 * fresh[0:1] + new1 * fresh[1:2]
    parts = [(peak + jnp.log2(total), mixed / total)]

    def columns(k):
        wh[k], wl[k] = split2(w[k])

    columns(0)
    arrived(w.at[1], CW)
    columns(1)
    arrived(w.at[2], YW)
    put(w.at[2], w.at[3], W_SEND, CYW, in_quad(1))
    sent(qbuf.at[pl.ds(0, 8)], A_SEND)
    sent(qbuf.at[pl.ds(0, 7)], A2_SEND)
    sent(kv.at[pl.ds(0, 3)], KV_SEND)

    def logs_of(values, j):
        return jnp.sum(jnp.where(lane16 == row16 + BLOCK * j, values, 0.0), axis=1, keepdims=True)

    parts.append((logs_of(osend[0, BLOCK:], 0), osend[0, :BLOCK]))
    arrived(orecv.at[pl.ds(1, Z - 1)], B_RECV)
    for s in range(1, Z):
        mine = Z - s
        parts.append((logs_of(orecv[s, BLOCK:], mine % 8), orecv[s, :BLOCK]))
    peak = parts[0][0]
    for logs, _ in parts[1:]:
        peak = jnp.maximum(peak, logs)
    total, mixed = jnp.zeros((BLOCK, 1), F32), jnp.zeros((BLOCK, HD), F32)
    for logs, value in parts:
        share = jnp.exp2(logs - peak)
        total += share
        mixed += share * value
    mine = pl.ds(pl.multiple_of(z * BLOCK, BLOCK), BLOCK)
    att[mine, :] = mixed / total

    for d in FAR_FIRST:
        put(att.at[mine], att.at[mine], C_SEND, C_RECV, along(d))
    sent(osend.at[pl.ds(1, Z - 1)], B_SEND)
    columns(2)
    arrived(w.at[3], CYW)
    columns(3)
    sent(w.at[pl.ds(0, 3)], W_SEND)
    arrived(att.at[pl.ds(0, (Z - 1) * BLOCK)], C_RECV)

    rows = jnp.concatenate([att[pl.ds(g, 32, stride=8), :] for g in range(8)], axis=1)
    high, low = split2(rows)
    halves = jnp.concatenate([high, low], axis=0)
    for k in (2, 3, 1, 0):
        part = nt(halves, wh[k])
        part = part[:32] + part[32:] + nt(high, wl[k])
        for h in range(HEADS):
            psend[k * HEADS + h, :, :80] = part[4 * h : 4 * h + 4]
        for d in (6, 5, 7, 4, 2, 1, 3, 0):
            if (k, d) != (0, 0):
                slot = ((d & 4) + (4 - (d & 3)) % 4) * QUAD + q
                put(psend.at[k * HEADS + head_of(d)], precv.at[slot], D_SEND, D_RECV, in_quad(k, d))
    precv[q] = psend[head]
    sent(att.at[pl.ds(0, (Z - 1) * BLOCK)], C_SEND)
    sent(psend.at[pl.ds(0, HEADS * QUAD - 1)], D_SEND)
    arrived(precv.at[pl.ds(0, HEADS * QUAD - 1)], D_RECV)
    for other in range(QUAD):
        summed = precv[other]
        for d in range(1, HEADS):
            summed += precv[d * QUAD + other]
        for half in range(2):
            for t in range(2):
                out_ref[t, half * QUAD + other, :] = summed[half * 2 + t, :80]


def local(
    queries, prompt_keys, prompt_values, suffix_keys, suffix_values, new_keys, new_values, suffix_lengths, out_weight
):
    return pl.pallas_call(
        kernel,
        out_shape=pltpu.VMEM((2, 8, 80), F32),
        in_specs=[pl.BlockSpec(memory_space=pltpu.HBM)] * 9,
        out_specs=pl.BlockSpec(memory_space=pltpu.VMEM),
        scratch_shapes=[
            pltpu.VMEM((Z, BLOCK, HD), F32),
            pltpu.VMEM((QUAD, 2, 256, HD), F32),
            pltpu.VMEM((QUAD, 80, 1024), F32),
            pltpu.VMEM((2, 128, HD), F32),
            pltpu.VMEM((2, 2, HD), F32),
            pltpu.SMEM((1,), jnp.int32),
            pltpu.VMEM((1024, 256), BF16),
            pltpu.VMEM((1024, 256), BF16),
            pltpu.VMEM((1024, 256), BF16),
            pltpu.VMEM((1024, 256), BF16),
            pltpu.VMEM((QUAD, 80, 1024), BF16),
            pltpu.VMEM((QUAD, 80, 1024), BF16),
            pltpu.VMEM((Z, BLOCK + 1, HD), F32),
            pltpu.VMEM((Z, BLOCK + 1, HD), F32),
            pltpu.VMEM((Z * BLOCK, HD), F32),
            pltpu.VMEM((QUAD * HEADS, 4, 128), F32),
            pltpu.VMEM((HEADS * QUAD, 4, 128), F32),
            pltpu.SemaphoreType.DMA((SEMS,)),
        ],
        compiler_params=pltpu.CompilerParams(
            collective_id=0, has_side_effects=True, vmem_limit_bytes=60 * 2**20
        ),
    )(
        queries.reshape(BLOCK, HD),
        prompt_keys.reshape(256, HD),
        prompt_values.reshape(256, HD),
        suffix_keys.reshape(128, HD),
        suffix_values.reshape(128, HD),
        new_keys.reshape(2, HD),
        new_values.reshape(2, HD),
        suffix_lengths,
        out_weight.T,
    )


def solution(mesh):
    return jax.shard_map(
        local,
        mesh=mesh,
        in_specs=(
            P(None, "ctx", "head", None),
            P("ctx", "head", None),
            P("ctx", "head", None),
            P("ctx", None, "head", None),
            P("ctx", None, "head", None),
            P(None, "ctx", "head", None),
            P(None, "ctx", "head", None),
            P("ctx"),
            P("head", "ctx"),
        ),
        out_specs=P(None, "head", "ctx"),
        check_vma=False,
    )
```
